512 devices in a mesh: group: 16 (over y, core), band: 32 (over x, z).
Axes of the slice: x: 4, y: 8, z: 8, core: 2. Of those that a mesh axis runs over, the one named last changes fastest.
Arguments:
- features: bfloat16 [131072, 256], P(('group', 'band')), may hold values from -6 to 6
- block_index: int32 [1024, 24], P(('group', 'band')), may hold values from 0 to 63
- block_count: int32 [1024], P(('group', 'band')), may hold values from 6 to 24, as said below
- block_values: bfloat16 [1024, 24, 128, 128], P(('group', 'band')), may hold values from -0.078125 to 0.078125
- cut_weight: bfloat16 [131072, 2048], P(('group', 'band')), may hold values from -0.078125 to 0.078125
- send_rows: int32 [512, 16, 128], P(('group', 'band')), may hold values from 0 to 255
- send_count: int32 [512, 16], P(('group', 'band')), may hold values from 32 to 128, as said below
- w_self: bfloat16 [256, 256], replicated, may hold values from -0.375 to 0.375
- w_neigh: bfloat16 [256, 256], replicated, may hold values from -0.375 to 0.375
- bias: float32 [256], replicated, may hold values from -3 to 3
- d_out: bfloat16 [131072, 256], P(('group', 'band')), may hold values from -6 to 6
Outputs:
- output: bfloat16 [131072, 256], P(('group', 'band'))
- d_features: bfloat16 [131072, 256], P(('group', 'band'))
- grad_blocks: bfloat16 [1024, 24, 128, 128], P(('group', 'band'))
- grad_self: float32 [256, 256], replicated
- grad_neigh: float32 [256, 256], replicated
- grad_bias: float32 [256], replicated
The draws below stay inside these ranges and needn't reach their ends.
Inputs may be any that keep to these rules, and one draw needn't show every extreme that they name: `block_count`: the first row tile has all 24 slots live. `send_count`: band p sends 128 live rows to group p % 16.
All inputs are finite; a program needn't handle non-finite values.
Results may differ from the reference program's by a relative error of at most 0.012.
Values may be sent and summed in bfloat16 or wider, within the bound.
No kernel may reach another device: no remote copies, remote signals or barrier semaphores. Data moves between devices by JAX's collectives and lax.ppermute only.
A program may use at most 64 MiB of HBM per device.

```python
import math
import jax
import jax.numpy as jnp
from jax import lax

F = 256
H = 256
TILE = 128
NODE_DEV = 256
K_BLK = 24
CUT = 128
TILES_DEV = 2
GROUP_TILES = 64
SENDERS = 512
NODES = 131072
TILES = 1024
CUT_COLS = 2048
N_GROUP = 16
N_BAND = 32


def draw_block_count(key, part):
    key = jax.random.fold_in(key, 11)
    counts = jax.random.randint(key, (TILES,), max(1, K_BLK // 4), K_BLK + 1)
    return counts.at[0].set(K_BLK).astype(jnp.int32)


def draw_send_count(key, part):
    key = jax.random.fold_in(key, 12)
    counts = jax.random.randint(key, (SENDERS, N_GROUP), max(1, CUT // 4), CUT + 1)
    senders = jnp.arange(SENDERS)
    return counts.at[senders, senders % N_GROUP].set(CUT).astype(jnp.int32)


def place_ends(result, rng, low, high):
    shape = result.shape
    spot = [jax.random.randint(jax.random.fold_in(rng, axis), (), 0, shape[axis]) for axis in range(len(shape))]
    result = result.at[tuple(spot)].set(low)
    longest = shape.index(max(shape))
    spot[longest] = (spot[longest] + 1) % shape[longest]
    return result.at[tuple(spot)].set(high)


def levels(rng, extent, split, least, top_value):
    level = 1.0
    for axis_at, blocks in split:
        heights = jax.random.uniform(jax.random.fold_in(jax.random.fold_in(rng, 6), axis_at), (blocks,), jnp.float32, least / len(split), top_value / len(split))
        level = level * jnp.repeat(jnp.exp(heights), extent[axis_at] // blocks).reshape((-1,) + (1,) * (len(extent) - 1 - axis_at))
    return level


def bell_draw(stream_key, shape, scale, limit, split=(), kind=jnp.bfloat16):
    gain = levels(stream_key, shape, split, -0.22, 0.18) if split else 1.0
    values = jax.random.normal(stream_key, shape, jnp.float32) * scale * gain
    return jnp.minimum(jnp.maximum(values, -limit), limit).astype(kind)


def setup_inputs(seed: int = 0) -> dict:
    keys = jax.random.split(jax.random.key(seed), 12)
    return {
        "features": bell_draw(keys[0], (NODES, F), 1.0, 6.0, ((0, 512),)),
        "block_index": place_ends(jax.random.randint(keys[1], (TILES, K_BLK), 0, GROUP_TILES), jax.random.fold_in(keys[1], 1), 0, GROUP_TILES - 1).astype(jnp.int32),
        "block_count": draw_block_count(jax.random.fold_in(keys[11], 71), 0),
        "block_values": bell_draw(keys[3], (TILES, K_BLK, TILE, TILE), (K_BLK * TILE + CUT_COLS) ** -0.5, 0.078125, ((0, 512),)),
        "cut_weight": bell_draw(keys[4], (NODES, CUT_COLS), (K_BLK * TILE + CUT_COLS) ** -0.5, 0.078125, ((0, 512),)),
        "send_rows": place_ends(jax.random.randint(keys[5], (SENDERS, N_GROUP, CUT), 0, NODE_DEV), jax.random.fold_in(keys[5], 1), 0, NODE_DEV - 1).astype(jnp.int32),
        "send_count": draw_send_count(jax.random.fold_in(keys[11], 71), 0),
        "w_self": bell_draw(keys[7], (F, H), F ** -0.5, 0.375),
        "w_neigh": bell_draw(keys[8], (F, H), F ** -0.5, 0.375),
        "bias": bell_draw(keys[9], (H,), 0.5, 3.0, (), jnp.float32),
        "d_out": bell_draw(keys[10], (NODES, H), 1.0, 6.0, ((0, 512),)),
    }


def reference(features, block_index, block_count, block_values, cut_weight, send_rows, send_count, w_self, w_neigh, bias, d_out):
    group_span = GROUP_TILES * TILE
    by_band = features.reshape(N_GROUP, N_BAND, NODE_DEV, F)
    lists = send_rows.reshape(N_GROUP, N_BAND, N_GROUP, CUT)
    counts = send_count.reshape(N_GROUP, N_BAND, N_GROUP)
    scale = 1.0 / math.sqrt(NODES)

    def step(carry, device):
        total, acc_self, acc_neigh, acc_bias = carry
        grp = device // N_BAND
        bnd = device % N_BAND
        rows = lax.dynamic_slice_in_dim(features, device * NODE_DEV, NODE_DEV, 0)
        group_rows = lax.dynamic_slice_in_dim(features, grp * group_span, group_span, 0)
        group_tiles = group_rows.reshape(GROUP_TILES, TILE, F)
        index_here = lax.dynamic_slice_in_dim(block_index, device * TILES_DEV, TILES_DEV, 0)
        count_here = lax.dynamic_slice_in_dim(block_count, device * TILES_DEV, TILES_DEV, 0)
        values_here = lax.dynamic_slice_in_dim(block_values, device * TILES_DEV, TILES_DEV, 0)
        live = jnp.arange(K_BLK)[None, :] < count_here[:, None]
        live_blocks = jnp.where(live[:, :, None, None], values_here, jnp.zeros_like(values_here))
        picked = group_tiles[index_here]
        inner = jnp.einsum('tkij,tkjf->tif', live_blocks.astype(jnp.float32), picked.astype(jnp.float32)).reshape(NODE_DEV, F)
        source_rows = lax.dynamic_index_in_dim(by_band, bnd, 1, keepdims=False)
        list_band = lax.dynamic_index_in_dim(lists, bnd, 1, keepdims=False)
        slot_rows = lax.dynamic_index_in_dim(list_band, grp, 1, keepdims=False)
        count_band = lax.dynamic_index_in_dim(counts, bnd, 1, keepdims=False)
        slot_count = lax.dynamic_index_in_dim(count_band, grp, 1, keepdims=False)
        slot_live = jnp.arange(CUT)[None, :] < slot_count[:, None]
        arrived = jnp.take_along_axis(source_rows, slot_rows[:, :, None], axis=1)
        arrived = jnp.where(slot_live[:, :, None], arrived, jnp.zeros_like(arrived))
        weights_here = lax.dynamic_slice_in_dim(cut_weight, device * NODE_DEV, NODE_DEV, 0)
        outer = jnp.dot(weights_here, arrived.reshape(CUT_COLS, F), preferred_element_type=jnp.float32)
        aggregate = (inner + outer).astype(jnp.bfloat16)
        pre = jnp.dot(rows, w_self, preferred_element_type=jnp.float32) + jnp.dot(aggregate, w_neigh, preferred_element_type=jnp.float32) + bias
        output = jax.nn.silu(pre).astype(jnp.bfloat16)
        cot = lax.dynamic_slice_in_dim(d_out, device * NODE_DEV, NODE_DEV, 0).astype(jnp.float32)
        sig = jax.nn.sigmoid(pre)
        d_pre = (cot * sig * (1.0 + pre * (1.0 - sig))).astype(jnp.bfloat16)
        acc_self = acc_self + jnp.dot(rows.T, d_pre, preferred_element_type=jnp.float32)
        acc_neigh = acc_neigh + jnp.dot(aggregate.T, d_pre, preferred_element_type=jnp.float32)
        acc_bias = acc_bias + lax.optimization_barrier(jnp.sum(d_pre.astype(jnp.float32), axis=0))
        d_aggregate = jnp.dot(d_pre, w_neigh.T, preferred_element_type=jnp.float32).astype(jnp.bfloat16)
        d_tiles = d_aggregate.reshape(TILES_DEV, TILE, F).astype(jnp.float32)
        block_grad = jnp.einsum('tif,tkjf->tkij', d_tiles, picked.astype(jnp.float32))
        block_grad = jnp.where(live[:, :, None, None], block_grad, jnp.zeros_like(block_grad)).astype(jnp.bfloat16)
        terms = jnp.einsum('tkij,tif->tkjf', live_blocks.astype(jnp.float32), d_tiles)
        band_term = jnp.zeros((GROUP_TILES, TILE, F), jnp.float32).at[index_here].add(terms)
        band_term = lax.optimization_barrier(band_term.astype(jnp.bfloat16)).astype(jnp.float32).reshape(group_span, F)
        current = lax.dynamic_slice_in_dim(total, grp * group_span, group_span, 0)
        total = lax.dynamic_update_slice_in_dim(total, current + band_term, grp * group_span, 0)
        self_term = jnp.dot(d_pre, w_self.T, preferred_element_type=jnp.float32)
        current = lax.dynamic_slice_in_dim(total, device * NODE_DEV, NODE_DEV, 0)
        total = lax.dynamic_update_slice_in_dim(total, current + self_term, device * NODE_DEV, 0)
        back_rows = jnp.dot(weights_here.T, d_aggregate, preferred_element_type=jnp.float32).astype(jnp.bfloat16)
        back_rows = back_rows.reshape(N_GROUP, CUT, F).astype(jnp.float32)
        back_rows = jnp.where(slot_live[:, :, None], back_rows, jnp.zeros_like(back_rows))
        senders = (jnp.arange(N_GROUP, dtype=jnp.int32) * N_BAND + bnd.astype(jnp.int32)) * NODE_DEV
        targets = (senders[:, None] + slot_rows.astype(jnp.int32)).reshape(CUT_COLS)
        total = total.at[targets].add(back_rows.reshape(CUT_COLS, F))
        return ((total, acc_self, acc_neigh, acc_bias), (output, block_grad))
    start = (jnp.zeros((NODES, F), jnp.float32), jnp.zeros((F, H), jnp.float32), jnp.zeros((F, H), jnp.float32), jnp.zeros((H,), jnp.float32))
    final, stacked = lax.scan(step, start, jnp.arange(SENDERS, dtype=jnp.int32))
    total, acc_self, acc_neigh, acc_bias = final
    output = stacked[0].reshape(NODES, H)
    grad_blocks = stacked[1].reshape(TILES, K_BLK, TILE, TILE)
    return (output, total.astype(jnp.bfloat16), grad_blocks, acc_self * scale, acc_neigh * scale, acc_bias * scale)
```

```python
import functools
import math

import jax
import jax.numpy as jnp
from jax import lax
from jax.experimental import pallas as pl
from jax.experimental.pallas import tpu as pltpu
from jax.sharding import Mesh, PartitionSpec as P

BF = jnp.bfloat16
F32 = jnp.float32
TN = (((0,), (0,)), ((), ()))
NT = (((1,), (1,)), ((), ()))
NX, NZ, NY, NC = 4, 8, 8, 2
NG = NY * NC
HALF = NX * NZ
GRAD_ROWS = 40
VMEM = pl.BlockSpec(memory_space=pltpu.VMEM)
SMEM = pl.BlockSpec(memory_space=pltpu.SMEM)
HBM = pl.BlockSpec(memory_space=pl.ANY)


def sds(shape, dtype):
    return jax.ShapeDtypeStruct(shape, dtype)


def call(body, out_shape, in_specs, out_specs, scratch=(), flops=0, nbytes=0, vmem=24):
    return pl.pallas_call(
        body,
        out_shape=out_shape,
        in_specs=in_specs,
        out_specs=out_specs,
        scratch_shapes=list(scratch),
        compiler_params=pltpu.CompilerParams(vmem_limit_bytes=vmem << 20),
        cost_estimate=pl.CostEstimate(flops=flops, bytes_accessed=nbytes, transcendentals=0),
    )


def hot_columns(rows_ref, count_ref, g, nodes):
    rows = rows_ref[g : g + 1, :]
    lane = lax.broadcasted_iota(jnp.int32, rows.shape, 1)
    rows = jnp.where(lane < count_ref[0, g], rows, -1)
    node = lax.broadcasted_iota(jnp.int32, (nodes, rows.shape[1]), 0)
    return jnp.where(node == rows, 1.0, 0.0).astype(BF)


def pick_body(count_ref, rows_ref, feat_ref, out_ref):
    feat = feat_ref[...]
    for g in range(out_ref.shape[0]):
        hot = hot_columns(rows_ref, count_ref, g, feat.shape[0])
        out_ref[g] = lax.dot_general(hot, feat, TN, preferred_element_type=F32).astype(BF)


def place(index_ref, count_ref, t, k):
    index = index_ref[t, k]
    band = lax.shift_right_logical(index, 1)
    even = (band & (NZ - 1)) * NX + lax.shift_right_logical(band, 3)
    slot = jnp.where((index & 1) == 0, even, HALF + band)
    return jnp.where(k < count_ref[t], slot, 2 * HALF)


def main_body(
    index_ref, count_ref, even_ref, odd_ref, blocks_ref, outer_ref, pre_ref, w_ref, dout_ref,
    out_ref, dpre_ref, dagg_ref, agg_ref, teven_ref, todd_ref,
    tiles, acc, sems,
):
    slots = blocks_ref.shape[1]
    copies = [
        pltpu.make_async_copy(even_ref, tiles.at[pl.ds(0, HALF)], sems.at[0]),
        pltpu.make_async_copy(odd_ref, tiles.at[pl.ds(HALF, HALF)], sems.at[1]),
    ]
    for copy in copies:
        copy.start()
    tiles[2 * HALF] = jnp.zeros(tiles.shape[1:], BF)

    def clear(i, carry):
        acc[i] = jnp.zeros(acc.shape[1:], F32)
        return carry

    lax.fori_loop(0, 2 * HALF, clear, 0)
    for copy in copies:
        copy.wait()
    where = [[place(index_ref, count_ref, t, k) for k in range(slots)] for t in range(2)]
    for t in range(2):
        rows = pl.ds(t * 128, 128)
        total = outer_ref[rows, :]
        for k in range(0, slots, 2):
            left = jnp.concatenate([blocks_ref[t, k], blocks_ref[t, k + 1]], axis=1)
            right = jnp.concatenate([tiles[where[t][k]], tiles[where[t][k + 1]]], axis=0)
            total = total + jnp.dot(left, right, preferred_element_type=F32)
        agg = total.astype(BF)
        agg_ref[rows, :] = agg
        pre = pre_ref[rows, :] + jnp.dot(agg, w_ref[...], preferred_element_type=F32)
        sig = jax.nn.sigmoid(pre)
        out_ref[rows, :] = (pre * sig).astype(BF)
        d_pre = (dout_ref[rows, :].astype(F32) * sig * (1.0 + pre * (1.0 - sig))).astype(BF)
        dpre_ref[rows, :] = d_pre
        d_agg = lax.dot_general(d_pre, w_ref[...], NT, preferred_element_type=F32).astype(BF)
        dagg_ref[rows, :] = d_agg
        for k in range(slots):
            spot = where[t][k]
            term = lax.dot_general(blocks_ref[t, k], d_agg, TN, preferred_element_type=F32)
            acc[spot] = acc[spot] + term

    def store(i, carry):
        teven_ref[i] = acc[i].astype(BF)
        todd_ref[i] = acc[HALF + i].astype(BF)
        return carry

    lax.fori_loop(0, HALF, store, 0)


def third_body(
    dagg_ref, dpre_ref, agg_ref, feat_ref, cut_ref, w_ref, back_ref, part_ref, self_ref
):
    d_pre = dpre_ref[...]
    width = d_pre.shape[1]
    part_ref[pl.ds(0, width), :] = lax.dot_general(
        feat_ref[...], d_pre, TN, preferred_element_type=F32
    )
    part_ref[pl.ds(width, width), :] = lax.dot_general(
        agg_ref[...], d_pre, TN, preferred_element_type=F32
    )
    rest = part_ref.shape[0] - 2 * width
    row = lax.broadcasted_iota(jnp.int32, (rest, width), 0)
    bias = jnp.sum(d_pre.astype(F32), axis=0, keepdims=True)
    part_ref[pl.ds(2 * width, rest), :] = jnp.where(row == 0, bias, 0.0)
    self_ref[...] = lax.dot_general(d_pre, w_ref[...], NT, preferred_element_type=F32)
    d_agg = dagg_ref[...]
    for c in range(0, cut_ref.shape[1], 256):
        back_ref[pl.ds(c, 256), :] = lax.dot_general(
            cut_ref[:, pl.ds(c, 256)], d_agg, TN, preferred_element_type=F32
        ).astype(BF)


def blocks_body(index_ref, count_ref, even_ref, odd_ref, dagg_ref, out_ref, tiles, sems):
    copies = [
        pltpu.make_async_copy(even_ref, tiles.at[pl.ds(0, HALF)], sems.at[0]),
        pltpu.make_async_copy(odd_ref, tiles.at[pl.ds(HALF, HALF)], sems.at[1]),
    ]
    for copy in copies:
        copy.start()
    tiles[2 * HALF] = jnp.zeros(tiles.shape[1:], BF)
    for copy in copies:
        copy.wait()
    for t in range(2):
        d_agg = dagg_ref[pl.ds(t * 128, 128), :]
        for k in range(out_ref.shape[1]):
            tile = tiles[place(index_ref, count_ref, t, k)]
            out_ref[t, k] = lax.dot_general(
                d_agg, tile, NT, preferred_element_type=F32
            ).astype(BF)


def base_body(count_ref, rows_ref, back_ref, self_ref, out_ref):
    total = self_ref[...]
    for g in range(0, back_ref.shape[0], 2):
        hot = jnp.concatenate(
            [hot_columns(rows_ref, count_ref, g + i, total.shape[0]) for i in range(2)], axis=1
        )
        rows = jnp.concatenate([back_ref[g], back_ref[g + 1]], axis=0)
        total = total + jnp.dot(hot, rows, preferred_element_type=F32)
    out_ref[...] = total


def a2a(x, axis):
    return lax.all_to_all(x, axis, 0, 0, tiled=True)


def spread(x, axis, n):
    return a2a(jnp.broadcast_to(x[None], (n, *x.shape)), axis)


def local(
    features, block_index, block_count, block_values, cut_weight, send_rows, send_count,
    w_self, w_neigh, bias, d_out,
):
    nodes, width = features.shape
    tiles_here, slots = block_index.shape
    scale = 1.0 / math.sqrt(nodes * NG * HALF)
    rows2 = send_rows.reshape(NG, -1)
    cut = rows2.shape[1]

    even = spread(features[:128], "x", NX)
    even = lax.all_gather(even, "z", axis=0, tiled=True)
    odd = spread(features[128:], "z", NZ)
    odd = spread(odd, "x", NX).reshape(HALF, 128, width)

    outgoing = call(
        pick_body, sds((NG, cut, width), BF), [SMEM, VMEM, VMEM], VMEM,
        flops=2 * NG * cut * width * nodes, nbytes=1 << 20,
    )(send_count, rows2, features)
    arrived = a2a(outgoing, ("y", "c")).reshape(NG * cut, width)
    outer = jnp.dot(cut_weight, arrived, preferred_element_type=F32)
    own_pre = jnp.dot(features, w_self, preferred_element_type=F32) + bias

    node_bf = sds((nodes, width), BF)
    half_bf = sds((HALF, 128, width), BF)
    gathered = pltpu.VMEM((2 * HALF + 1, 128, width), BF)
    output, d_pre, d_agg, aggregate, t_even, t_odd = call(
        main_body,
        (node_bf, node_bf, node_bf, node_bf, half_bf, half_bf),
        [SMEM, SMEM, HBM, HBM, VMEM, VMEM, VMEM, VMEM, VMEM],
        (VMEM,) * 6,
        [gathered, pltpu.VMEM((2 * HALF + 1, 128, width), F32), pltpu.SemaphoreType.DMA((2,))],
        flops=2 << 30, nbytes=16 << 20, vmem=40,
    )(block_index, block_count, even, odd, block_values, outer, own_pre, w_neigh, d_out)

    t_even = lax.psum_scatter(t_even.reshape(NZ, NX * 128, width), "z", scatter_dimension=0)
    t_odd = a2a(t_odd.reshape(NX, NZ, 128, width), "x")
    t_odd = jnp.sum(t_odd.astype(F32), axis=0).astype(BF)
    t_odd = a2a(t_odd, "z")
    t_odd = jnp.sum(t_odd.astype(F32), axis=0)
    t_even = a2a(t_even.reshape(NX, 128, width), "x")
    t_even = jnp.sum(t_even.astype(F32), axis=0)

    back, part, self_back = call(
        third_body,
        (sds((NG * cut, width), BF), sds((NG * GRAD_ROWS, width), F32), sds((nodes, width), F32)),
        [VMEM] * 6, (VMEM,) * 3, flops=400 << 20, nbytes=4 << 20,
    )(d_agg, d_pre, aggregate, features, cut_weight, w_self)
    returned = a2a(back.reshape(NG, cut, width), ("y", "c"))
    base = call(
        base_body, sds((nodes, width), F32), [SMEM, VMEM, VMEM, VMEM], VMEM,
        flops=2 * NG * cut * width * nodes, nbytes=2 << 20,
    )(send_count, rows2, returned, self_back)
    d_features = (base + jnp.concatenate([t_even, t_odd], axis=0)).astype(BF)

    part = jnp.sum(a2a(part.reshape(NG, GRAD_ROWS, width), ("y", "c")), axis=0)
    part = jnp.sum(spread(part, "x", NX), axis=0)
    part = jnp.sum(spread(part, "z", NZ), axis=0) * scale
    grads = spread(part, ("y", "c"), NG).reshape(-1, width)

    grad_blocks = call(
        blocks_body, sds(block_values.shape, BF), [SMEM, SMEM, HBM, HBM, VMEM], VMEM,
        [gathered, pltpu.SemaphoreType.DMA((2,))],
        flops=2 * tiles_here * slots * 128 * 128 * width, nbytes=6 << 20,
    )(block_index, block_count, even, odd, d_agg)

    return (
        output,
        d_features,
        grad_blocks,
        grads[:width],
        grads[width : 2 * width],
        grads[2 * width],
    )


def solution(mesh):
    mesh = Mesh(mesh.devices.reshape(NY, NC, NX, NZ), ("y", "c", "x", "z"))
    rows = ("y", "c", "x", "z")
    split = [P(rows)] * 7 + [P()] * 3 + [P(rows)]
    return jax.shard_map(
        local,
        mesh=mesh,
        in_specs=tuple(split),
        out_specs=(P(rows), P(rows), P(rows), P(), P(), P()),
        check_vma=False,
    )
```

```python
import functools
import math

import jax
import jax.numpy as jnp
from jax import lax
from jax.experimental import pallas as pl
from jax.experimental.pallas import tpu as pltpu
from jax.sharding import Mesh, PartitionSpec as P

BF = jnp.bfloat16
F32 = jnp.float32
TN = (((0,), (0,)), ((), ()))
NT = (((1,), (1,)), ((), ()))
NX, NZ, NY, NC = 4, 8, 8, 2
NG = NY * NC
HALF = NX * NZ
GRAD_ROWS = 40
VMEM = pl.BlockSpec(memory_space=pltpu.VMEM)
SMEM = pl.BlockSpec(memory_space=pltpu.SMEM)
HBM = pl.BlockSpec(memory_space=pl.ANY)


def sds(shape, dtype):
    return jax.ShapeDtypeStruct(shape, dtype)


def call(body, out_shape, in_specs, out_specs, scratch=(), flops=0, nbytes=0, vmem=24):
    return pl.pallas_call(
        body,
        out_shape=out_shape,
        in_specs=in_specs,
        out_specs=out_specs,
        scratch_shapes=list(scratch),
        compiler_params=pltpu.CompilerParams(vmem_limit_bytes=vmem << 20),
        cost_estimate=pl.CostEstimate(flops=flops, bytes_accessed=nbytes, transcendentals=0),
    )


def hot_columns(rows_ref, count_ref, g, nodes):
    rows = rows_ref[g : g + 1, :]
    lane = lax.broadcasted_iota(jnp.int32, rows.shape, 1)
    rows = jnp.where(lane < count_ref[0, g], rows, -1)
    node = lax.broadcasted_iota(jnp.int32, (nodes, rows.shape[1]), 0)
    return jnp.where(node == rows, 1.0, 0.0).astype(BF)


def pick_body(count_ref, rows_ref, feat_ref, out_ref):
    feat = feat_ref[...]
    for g in range(out_ref.shape[0]):
        hot = hot_columns(rows_ref, count_ref, g, feat.shape[0])
        out_ref[g] = lax.dot_general(hot, feat, TN, preferred_element_type=F32).astype(BF)


def band_of(index_ref, t, k):
    index = index_ref[t, k]
    band = lax.shift_right_logical(index, 1)
    return lax.shift_right_logical(band, 3), band & (NZ - 1), index & 1


def tile_spot(index_ref, count_ref, my_x, t, k):
    x, z, odd = band_of(index_ref, t, k)
    spot = jnp.where(odd == 0, z * NX + x, HALF + ((x - my_x) & (NX - 1)) * NZ + z)
    return jnp.where(k < count_ref[t], spot, 2 * HALF)


def term_spot(index_ref, count_ref, t, k):
    x, z, odd = band_of(index_ref, t, k)
    return jnp.where(k < count_ref[t], (z * NX + x) * 2 + odd, 2 * HALF)


def fetch_tiles(sources, tiles, sems):
    starts = (0, HALF, HALF + NZ, HALF + 2 * NZ, HALF + 2 * NZ + NZ // 2, HALF + 3 * NZ)
    copies = [
        pltpu.make_async_copy(source, tiles.at[pl.ds(start, source.shape[0])], sems.at[i])
        for i, (source, start) in enumerate(zip(sources, starts, strict=True))
    ]
    for copy in copies:
        copy.start()
    tiles[2 * HALF] = jnp.zeros(tiles.shape[1:], BF)
    return copies


def main_body(
    index_ref, count_ref, x_ref, s0, s1, s2, s3, s4, s5, blocks_ref, outer_ref, pre_ref, w_ref, dout_ref,
    out_ref, dpre_ref, dagg_ref, agg_ref, term_ref,
    tiles, acc, sems,
):
    slots = blocks_ref.shape[1]
    copies = fetch_tiles((s0, s1, s2, s3, s4, s5), tiles, sems)

    def clear(i, carry):
        acc[i] = jnp.zeros(acc.shape[1:], F32)
        return carry

    lax.fori_loop(0, 2 * HALF, clear, 0)
    for copy in copies:
        copy.wait()
    my_x = x_ref[0]
    for t in range(2):
        where = [tile_spot(index_ref, count_ref, my_x, t, k) for k in range(slots)]
        rows = pl.ds(t * 128, 128)
        total = outer_ref[rows, :]
        for k in range(0, slots, 2):
            left = jnp.concatenate([blocks_ref[t, k], blocks_ref[t, k + 1]], axis=1)
            right = jnp.concatenate([tiles[where[k]], tiles[where[k + 1]]], axis=0)
            total = total + jnp.dot(left, right, preferred_element_type=F32)
        agg = total.astype(BF)
        agg_ref[rows, :] = agg
        pre = pre_ref[rows, :] + jnp.dot(agg, w_ref[...], preferred_element_type=F32)
        sig = jax.nn.sigmoid(pre)
        out_ref[rows, :] = (pre * sig).astype(BF)
        d_pre = (dout_ref[rows, :].astype(F32) * sig * (1.0 + pre * (1.0 - sig))).astype(BF)
        dpre_ref[rows, :] = d_pre
        d_agg = lax.dot_general(d_pre, w_ref[...], NT, preferred_element_type=F32).astype(BF)
        dagg_ref[rows, :] = d_agg
        for k in range(slots):
            spot = term_spot(index_ref, count_ref, t, k)
            term = lax.dot_general(blocks_ref[t, k], d_agg, TN, preferred_element_type=F32)
            acc[spot] = acc[spot] + term

    def store(i, carry):
        term_ref[i] = acc[i].astype(BF)
        return carry

    lax.fori_loop(0, 2 * HALF, store, 0)


def third_body(
    dagg_ref, dpre_ref, agg_ref, feat_ref, cut_ref, w_ref, back_ref, part_ref, self_ref
):
    d_pre = dpre_ref[...]
    width = d_pre.shape[1]
    part_ref[pl.ds(0, width), :] = lax.dot_general(
        feat_ref[...], d_pre, TN, preferred_element_type=F32
    )
    part_ref[pl.ds(width, width), :] = lax.dot_general(
        agg_ref[...], d_pre, TN, preferred_element_type=F32
    )
    rest = part_ref.shape[0] - 2 * width
    row = lax.broadcasted_iota(jnp.int32, (rest, width), 0)
    bias = jnp.sum(d_pre.astype(F32), axis=0, keepdims=True)
    part_ref[pl.ds(2 * width, rest), :] = jnp.where(row == 0, bias, 0.0)
    self_ref[...] = lax.dot_general(d_pre, w_ref[...], NT, preferred_element_type=F32)
    d_agg = dagg_ref[...]
    for c in range(0, cut_ref.shape[1], 256):
        back_ref[pl.ds(c, 256), :] = lax.dot_general(
            cut_ref[:, pl.ds(c, 256)], d_agg, TN, preferred_element_type=F32
        ).astype(BF)


def blocks_body(
    index_ref, count_ref, x_ref, s0, s1, s2, s3, s4, s5, dagg_ref, out_ref, tiles, sems
):
    copies = fetch_tiles((s0, s1, s2, s3, s4, s5), tiles, sems)
    my_x = x_ref[0]
    for copy in copies:
        copy.wait()
    for t in range(2):
        d_agg = dagg_ref[pl.ds(t * 128, 128), :]
        for k in range(out_ref.shape[1]):
            tile = tiles[tile_spot(index_ref, count_ref, my_x, t, k)]
            out_ref[t, k] = lax.dot_general(
                d_agg, tile, NT, preferred_element_type=F32
            ).astype(BF)


def base_body(count_ref, rows_ref, back_ref, self_ref, out_ref):
    total = self_ref[...]
    for g in range(0, back_ref.shape[0], 2):
        hot = jnp.concatenate(
            [hot_columns(rows_ref, count_ref, g + i, total.shape[0]) for i in range(2)], axis=1
        )
        rows = jnp.concatenate([back_ref[g], back_ref[g + 1]], axis=0)
        total = total + jnp.dot(hot, rows, preferred_element_type=F32)
    out_ref[...] = total


def a2a(x, axis):
    return lax.all_to_all(x, axis, 0, 0, tiled=True)


def spread(x, axis, n):
    return a2a(jnp.broadcast_to(x[None], (n, *x.shape)), axis)


def shift(x, axis, n, by):
    return lax.ppermute(x, axis, [(i, (i + by) % n) for i in range(n)])


def local(
    features, block_index, block_count, block_values, cut_weight, send_rows, send_count,
    w_self, w_neigh, bias, d_out,
):
    nodes, width = features.shape
    tiles_here, slots = block_index.shape
    scale = 1.0 / math.sqrt(nodes * NG * HALF)
    rows2 = send_rows.reshape(NG, -1)
    cut = rows2.shape[1]

    even = spread(features[:128], "x", NX)
    even = lax.all_gather(even, "z", axis=0, tiled=True)
    own = lax.all_gather(features[128:], "z", axis=0)
    left = shift(own, "x", NX, 1)
    right = shift(own, "x", NX, -1)
    far_low = shift(left[: NZ // 2], "x", NX, 1)
    far_high = shift(right[NZ // 2 :], "x", NX, -1)
    gathered = (even, own, right, far_low, far_high, left)
    my_x = lax.axis_index("x").astype(jnp.int32).reshape(1)

    outgoing = call(
        pick_body, sds((NG, cut, width), BF), [SMEM, VMEM, VMEM], VMEM,
        flops=2 * NG * cut * width * nodes, nbytes=1 << 20,
    )(send_count, rows2, features)
    arrived = a2a(outgoing, ("y", "c")).reshape(NG * cut, width)
    outer = jnp.dot(cut_weight, arrived, preferred_element_type=F32)
    own_pre = jnp.dot(features, w_self, preferred_element_type=F32) + bias

    node_bf = sds((nodes, width), BF)
    tile_scratch = pltpu.VMEM((2 * HALF + 1, 128, width), BF)
    copy_sems = pltpu.SemaphoreType.DMA((6,))
    output, d_pre, d_agg, aggregate, terms = call(
        main_body,
        (node_bf, node_bf, node_bf, node_bf, sds((2 * HALF, 128, width), BF)),
        [SMEM] * 3 + [HBM] * 6 + [VMEM] * 5,
        (VMEM,) * 5,
        [tile_scratch, pltpu.VMEM((2 * HALF + 1, 128, width), F32), copy_sems],
        flops=2 << 30, nbytes=16 << 20, vmem=40,
    )(block_index, block_count, my_x, *gathered, block_values, outer, own_pre, w_neigh, d_out)

    terms = lax.psum_scatter(terms.reshape(NZ, NX * nodes, width), "z", scatter_dimension=0)
    terms = a2a(terms.reshape(NX, nodes, width), "x")

    back, part, self_back = call(
        third_body,
        (sds((NG * cut, width), BF), sds((NG * GRAD_ROWS, width), F32), sds((nodes, width), F32)),
        [VMEM] * 6, (VMEM,) * 3, flops=400 << 20, nbytes=4 << 20,
    )(d_agg, d_pre, aggregate, features, cut_weight, w_self)
    returned = a2a(back.reshape(NG, cut, width), ("y", "c"))
    base = call(
        base_body, sds((nodes, width), F32), [SMEM, VMEM, VMEM, VMEM], VMEM,
        flops=2 * NG * cut * width * nodes, nbytes=2 << 20,
    )(send_count, rows2, returned, self_back)
    d_features = (base + jnp.sum(terms.astype(F32), axis=0)).astype(BF)

    part = jnp.sum(a2a(part.reshape(NC, NY * GRAD_ROWS, width), "c"), axis=0)
    part = jnp.sum(a2a(part.reshape(NY, GRAD_ROWS, width), "y"), axis=0)
    part = jnp.sum(lax.all_gather(part, "x", axis=0), axis=0)
    part = jnp.sum(lax.all_gather(part, "z", axis=0), axis=0) * scale
    part = lax.all_gather(part, "y", axis=0, tiled=True)
    grads = lax.all_gather(part, "c", axis=0, tiled=True)

    grad_blocks = call(
        blocks_body, sds(block_values.shape, BF), [SMEM] * 3 + [HBM] * 6 + [VMEM], VMEM,
        [tile_scratch, copy_sems],
        flops=2 * tiles_here * slots * 128 * 128 * width, nbytes=6 << 20,
    )(block_index, block_count, my_x, *gathered, d_agg)

    return (
        output,
        d_features,
        grad_blocks,
        grads[:width],
        grads[width : 2 * width],
        grads[2 * width],
    )


def solution(mesh):
    mesh = Mesh(mesh.devices.reshape(NY, NC, NX, NZ), ("y", "c", "x", "z"))
    rows = ("y", "c", "x", "z")
    split = [P(rows)] * 7 + [P()] * 3 + [P(rows)]
    return jax.shard_map(
        local,
        mesh=mesh,
        in_specs=tuple(split),
        out_specs=(P(rows), P(rows), P(rows), P(), P(), P()),
        check_vma=False,
    )
```

```python
import math

import jax
import jax.numpy as jnp
from jax import lax
from jax.experimental import pallas as pl
from jax.experimental.pallas import tpu as pltpu
from jax.sharding import Mesh, PartitionSpec as P

BF = jnp.bfloat16
F32 = jnp.float32
TN = (((0,), (0,)), ((), ()))
NT = (((1,), (1,)), ((), ()))
NX, NZ, NY, NC = 4, 8, 8, 2
NG = NY * NC
BANDS = NX * NZ
GRAD_ROWS = 40
STORE = 8
VMEM = pl.BlockSpec(memory_space=pltpu.VMEM)
SMEM = pl.BlockSpec(memory_space=pltpu.SMEM)
HBM = pl.BlockSpec(memory_space=pl.ANY)


def sds(shape, dtype):
    return jax.ShapeDtypeStruct(shape, dtype)


def call(body, scalars, arrays, outs, out_specs=None, scratch=(), extra=(), flops=0, vmem=24):
    count, first = len(arrays), len(scalars)

    def kernel(*refs):
        sources = refs[first : first + count]
        rest = refs[first + count + len(extra) :]
        outputs, rest = rest[: len(outs)], rest[len(outs) :]
        buffers, sems, rest = rest[:count], rest[count], rest[count + 1 :]
        copies = [
            pltpu.make_async_copy(source, buffer, sems.at[i])
            for i, (source, buffer) in enumerate(zip(sources, buffers, strict=True))
        ]
        for copy in copies:
            copy.start()
        body(refs[:first], buffers, copies, outputs, *rest)

    nbytes = sum(a.size * a.dtype.itemsize for a in (*arrays, *outs))
    return pl.pallas_call(
        kernel,
        out_shape=tuple(outs),
        in_specs=[SMEM] * first + [HBM] * (count + len(extra)),
        out_specs=tuple(out_specs or [VMEM] * len(outs)),
        scratch_shapes=[
            *(pltpu.VMEM(a.shape, a.dtype) for a in arrays),
            pltpu.SemaphoreType.DMA((count,)),
            *scratch,
        ],
        compiler_params=pltpu.CompilerParams(vmem_limit_bytes=vmem << 20),
        cost_estimate=pl.CostEstimate(flops=flops, bytes_accessed=nbytes, transcendentals=0),
    )(*scalars, *arrays, *extra)


def wait(copies):
    for copy in copies:
        copy.wait()


def hot_columns(rows_ref, count_ref, g, nodes):
    rows = rows_ref[g : g + 1, :]
    lane = lax.broadcasted_iota(jnp.int32, rows.shape, 1)
    rows = jnp.where(lane < count_ref[0, g], rows, -1)
    node = lax.broadcasted_iota(jnp.int32, (nodes, rows.shape[1]), 0)
    return jnp.where(node == rows, 1.0, 0.0).astype(BF)


def pick_body(scalars, arrays, copies, outs):
    (count_ref,), (rows_ref, feat_ref), (out_ref,) = scalars, arrays, outs
    wait(copies)
    feat = feat_ref[...]
    for g in range(out_ref.shape[0]):
        hot = hot_columns(rows_ref, count_ref, g, feat.shape[0])
        out_ref[g] = lax.dot_general(hot, feat, TN, preferred_element_type=F32).astype(BF)


def spot_of(index_ref, count_ref, t, k):
    index = index_ref[t, k]
    z, x = lax.shift_right_logical(index, 1) & (NZ - 1), lax.shift_right_logical(index, 4)
    return jnp.where(k < count_ref[t], (z * NX + x) * 2 + (index & 1), 2 * BANDS)


def main_body(scalars, arrays, copies, outs, tiles, acc, terms, tile_sem, term_sems):
    index_ref, count_ref = scalars
    blocks_ref, outer_ref, pre_ref, w_ref, dout_ref = arrays[:5]
    out_ref, dpre_ref, dagg_ref, agg_ref, term_ref = outs
    slots = blocks_ref.shape[1]
    spare = 2 * BANDS
    tiles[spare] = jnp.zeros(tiles.shape[1:], BF)

    def clear(i, carry):
        acc[i] = jnp.zeros(acc.shape[1:], F32)
        return carry

    lax.fori_loop(0, spare, clear, 0)
    wait(copies)
    for t in range(2):
        rows = pl.ds(t * 128, 128)
        spots = [spot_of(index_ref, count_ref, t, k) for k in range(slots)]
        total = outer_ref[rows, :]
        for k in range(0, slots, 2):
            left = jnp.concatenate([blocks_ref[t, k], blocks_ref[t, k + 1]], axis=1)
            right = jnp.concatenate([tiles[spots[k]], tiles[spots[k + 1]]], axis=0)
            total = total + jnp.dot(left, right, preferred_element_type=F32)
        agg = total.astype(BF)
        agg_ref[rows, :] = agg
        pre = pre_ref[rows, :] + jnp.dot(agg, w_ref[...], preferred_element_type=F32)
        sig = jax.nn.sigmoid(pre)
        out_ref[rows, :] = (pre * sig).astype(BF)
        d_pre = (dout_ref[rows, :].astype(F32) * sig * (1.0 + pre * (1.0 - sig))).astype(BF)
        dpre_ref[rows, :] = d_pre
        d_agg = lax.dot_general(d_pre, w_ref[...], NT, preferred_element_type=F32).astype(BF)
        dagg_ref[rows, :] = d_agg
        for k in range(slots):
            term = lax.dot_general(blocks_ref[t, k], d_agg, TN, preferred_element_type=F32)
            acc[spots[k]] = acc[spots[k]] + term
    stores = []
    for c in range(STORE):
        part = pl.ds(c * (spare // STORE), spare // STORE)

        def convert(i, carry):
            terms[i] = acc[i].astype(BF)
            return carry

        lax.fori_loop(part.start, part.start + part.size, convert, 0)
        store = pltpu.make_async_copy(terms.at[part], term_ref.at[part], term_sems.at[c])
        store.start()
        stores.append(store)
    wait(stores)


def main_kernel(scalars, arrays, gathered, outs):
    count = len(arrays)

    def kernel(*refs):
        scalar_refs, refs = refs[:2], refs[2:]
        sources, gathered_ref, refs = refs[:count], refs[count], refs[count + 1 :]
        outputs, refs = refs[: len(outs)], refs[len(outs) :]
        buffers, (sems, tiles, acc, terms, tile_sem, term_sems) = refs[:count], refs[count:]
        copies = [pltpu.make_async_copy(gathered_ref, tiles.at[pl.ds(0, 2 * BANDS)], tile_sem)] + [
            pltpu.make_async_copy(source, buffer, sems.at[i])
            for i, (source, buffer) in enumerate(zip(sources, buffers, strict=True))
        ]
        for copy in copies:
            copy.start()
        main_body(scalar_refs, buffers, copies, outputs, tiles, acc, terms, tile_sem, term_sems)

    shape = (2 * BANDS + 1, *gathered.shape[1:])
    return pl.pallas_call(
        kernel,
        out_shape=tuple(outs),
        in_specs=[SMEM] * 2 + [HBM] * (count + 1),
        out_specs=(VMEM,) * (len(outs) - 1) + (HBM,),
        scratch_shapes=[
            *(pltpu.VMEM(a.shape, a.dtype) for a in arrays),
            pltpu.SemaphoreType.DMA((count,)),
            pltpu.VMEM(shape, BF),
            pltpu.VMEM(shape, F32),
            pltpu.VMEM(gathered.shape, BF),
            pltpu.SemaphoreType.DMA,
            pltpu.SemaphoreType.DMA((STORE,)),
        ],
        compiler_params=pltpu.CompilerParams(vmem_limit_bytes=40 << 20),
        cost_estimate=pl.CostEstimate(flops=1 << 30, bytes_accessed=12 << 20, transcendentals=0),
    )(*scalars, *arrays, gathered)


def third_body(scalars, arrays, copies, outs):
    dpre_ref, agg_ref, feat_ref, w_ref = arrays
    part_ref, self_ref = outs
    wait(copies)
    d_pre = dpre_ref[...]
    width = d_pre.shape[1]
    part_ref[pl.ds(0, width), :] = lax.dot_general(
        feat_ref[...], d_pre, TN, preferred_element_type=F32
    )
    part_ref[pl.ds(width, width), :] = lax.dot_general(
        agg_ref[...], d_pre, TN, preferred_element_type=F32
    )
    rest = part_ref.shape[0] - 2 * width
    row = lax.broadcasted_iota(jnp.int32, (rest, width), 0)
    bias = jnp.sum(d_pre.astype(F32), axis=0, keepdims=True)
    part_ref[pl.ds(2 * width, rest), :] = jnp.where(row == 0, bias, 0.0)
    self_ref[...] = lax.dot_general(d_pre, w_ref[...], NT, preferred_element_type=F32)


def back_body(scalars, arrays, copies, outs):
    (cut_ref, dagg_ref), (back_ref,) = arrays, outs
    wait(copies)
    d_agg = dagg_ref[...]
    cut = back_ref.shape[1]
    for g in range(0, back_ref.shape[0], 2):
        rows = lax.dot_general(
            cut_ref[:, pl.ds(g * cut, 2 * cut)], d_agg, TN, preferred_element_type=F32
        ).astype(BF)
        back_ref[g] = rows[:cut]
        back_ref[g + 1] = rows[cut:]


def blocks_body(scalars, arrays, copies, outs):
    (index_ref, count_ref), (tiles, dagg_ref), (out_ref,) = scalars, arrays, outs
    wait(copies)
    for t in range(2):
        d_agg = dagg_ref[pl.ds(t * 128, 128), :]
        for k in range(out_ref.shape[1]):
            live = k < count_ref[t]
            spot = jnp.where(live, spot_of(index_ref, count_ref, t, k), 0)

            @pl.when(live)
            def _(t=t, k=k, spot=spot, d_agg=d_agg):
                out_ref[t, k] = lax.dot_general(
                    d_agg, tiles[spot], NT, preferred_element_type=F32
                ).astype(BF)

            @pl.when(jnp.logical_not(live))
            def _(t=t, k=k):
                out_ref[t, k] = jnp.zeros(out_ref.shape[2:], BF)


def base_body(scalars, arrays, copies, outs):
    (count_ref,), (rows_ref, back_ref, self_ref), (out_ref,) = scalars, arrays, outs
    wait(copies)
    total = self_ref[...]
    for g in range(0, back_ref.shape[0], 2):
        hot = jnp.concatenate(
            [hot_columns(rows_ref, count_ref, g + i, total.shape[0]) for i in range(2)], axis=1
        )
        rows = jnp.concatenate([back_ref[g], back_ref[g + 1]], axis=0)
        total = total + jnp.dot(hot, rows, preferred_element_type=F32)
    out_ref[...] = total


def a2a(x, axis):
    return lax.all_to_all(x, axis, 0, 0, tiled=True)


def spread(x, axis, n):
    return a2a(jnp.broadcast_to(x[None], (n, *x.shape)), axis)


def shift(x, axis, n, by):
    return lax.ppermute(x, axis, [(i, (i + by) % n) for i in range(n)])


def local(
    features, block_index, block_count, block_values, cut_weight, send_rows, send_count,
    w_self, w_neigh, bias, d_out,
):
    nodes, width = features.shape
    tiles_here, slots = block_index.shape
    scale = 1.0 / math.sqrt(nodes * NG * BANDS)
    rows2 = send_rows.reshape(NG, -1)
    cut = rows2.shape[1]
    node_bf, node_f32 = sds((nodes, width), BF), sds((nodes, width), F32)
    cut_bf = sds((NG, cut, width), BF)

    gathered = lax.all_gather(features, "x", axis=0, tiled=True)
    gathered = lax.all_gather(gathered, "z", axis=0, tiled=True).reshape(2 * BANDS, 128, width)

    (outgoing,) = call(
        pick_body, [send_count], [rows2, features], [cut_bf], flops=2 * NG * cut * width * nodes
    )
    arrived = a2a(outgoing, ("y", "c")).reshape(NG * cut, width)
    outer = jnp.dot(cut_weight, arrived, preferred_element_type=F32)
    own_pre = jnp.dot(features, w_self, preferred_element_type=F32) + bias

    output, d_pre, d_agg, aggregate, terms = main_kernel(
        [block_index, block_count],
        [block_values, outer, own_pre, w_neigh, d_out],
        gathered,
        [node_bf, node_bf, node_bf, node_bf, sds(gathered.shape, BF)],
    )

    terms = lax.psum_scatter(terms.reshape(NZ, NX * nodes, width), "z", scatter_dimension=0)
    terms = terms.reshape(NX, nodes, width)
    me = lax.axis_index("x")
    own_back = lax.dynamic_index_in_dim(terms, me, 0, keepdims=False).astype(F32)
    for by in range(1, NX):
        away = lax.dynamic_index_in_dim(terms, (me + by) & (NX - 1), 0, keepdims=False)
        own_back = own_back + shift(away, "x", NX, by).astype(F32)

    part, self_back = call(
        third_body, [], [d_pre, aggregate, features, w_self],
        [sds((NG * GRAD_ROWS, width), F32), node_f32], flops=100 << 20,
    )
    part = jnp.sum(a2a(part.reshape(NC, NY * GRAD_ROWS, width), "c"), axis=0)
    part = jnp.sum(a2a(part.reshape(NY, GRAD_ROWS, width), "y"), axis=0)
    part = jnp.sum(spread(part, "x", NX), axis=0)
    part = jnp.sum(spread(part, "z", NZ), axis=0) * scale

    (back,) = call(
        back_body, [], [cut_weight, d_agg], [cut_bf], extra=[part],
        flops=2 * NG * cut * width * nodes,
    )
    returned = a2a(back, ("y", "c"))
    part = lax.all_gather(part, "y", axis=0, tiled=True)
    grads = lax.all_gather(part, "c", axis=0, tiled=True)
    (base,) = call(
        base_body, [send_count], [rows2, returned, self_back], [node_f32],
        flops=2 * NG * cut * width * nodes,
    )
    d_features = (base + own_back).astype(BF)

    (grad_blocks,) = call(
        blocks_body, [block_index, block_count], [gathered, d_agg], [sds(block_values.shape, BF)],
        extra=[part], flops=2 * tiles_here * slots * 128 * 128 * width,
    )

    return (
        output,
        d_features,
        grad_blocks,
        grads[:width],
        grads[width : 2 * width],
        grads[2 * width],
    )


def solution(mesh):
    mesh = Mesh(mesh.devices.reshape(NY, NC, NX, NZ), ("y", "c", "x", "z"))
    rows = ("y", "c", "x", "z")
    split = [P(rows)] * 7 + [P()] * 3 + [P(rows)]
    return jax.shard_map(
        local,
        mesh=mesh,
        in_specs=tuple(split),
        out_specs=(P(rows), P(rows), P(rows), P(), P(), P()),
        check_vma=False,
    )
```

```python
import math

import jax
import jax.numpy as jnp
from jax import lax
from jax.experimental import pallas as pl
from jax.experimental.pallas import tpu as pltpu
from jax.sharding import Mesh, PartitionSpec as P

BF = jnp.bfloat16
F32 = jnp.float32
TN = (((0,), (0,)), ((), ()))
NT = (((1,), (1,)), ((), ()))
NX, NZ, NY, NC = 4, 8, 8, 2
NG = NY * NC
BANDS = NX * NZ
GRAD_ROWS = 48
STORE = 8
VMEM = pl.BlockSpec(memory_space=pltpu.VMEM)
SMEM = pl.BlockSpec(memory_space=pltpu.SMEM)
HBM = pl.BlockSpec(memory_space=pltpu.HBM)


def sds(shape, dtype):
    return jax.ShapeDtypeStruct(shape, dtype)


def call(body, scalars, arrays, outs, out_specs=None, scratch=(), extra=(), flops=0, vmem=60):
    count, first = len(arrays), len(scalars)

    def kernel(*refs):
        sources = refs[first : first + count]
        rest = refs[first + count + len(extra) :]
        outputs, rest = rest[: len(outs)], rest[len(outs) :]
        buffers, sems, rest = rest[:count], rest[count], rest[count + 1 :]
        copies = [
            pltpu.make_async_copy(source, buffer, sems.at[i])
            for i, (source, buffer) in enumerate(zip(sources, buffers, strict=True))
        ]
        for copy in copies:
            copy.start()
        body(refs[:first], buffers, copies, outputs, *rest)

    nbytes = sum(a.size * a.dtype.itemsize for a in (*arrays, *outs))
    return pl.pallas_call(
        kernel,
        out_shape=tuple(outs),
        in_specs=[SMEM] * first + [HBM] * (count + len(extra)),
        out_specs=tuple(out_specs or [VMEM] * len(outs)),
        scratch_shapes=[
            *(pltpu.VMEM(a.shape, a.dtype) for a in arrays),
            pltpu.SemaphoreType.DMA((count,)),
            *scratch,
        ],
        compiler_params=pltpu.CompilerParams(vmem_limit_bytes=vmem << 20),
        cost_estimate=pl.CostEstimate(flops=flops, bytes_accessed=nbytes, transcendentals=0),
    )(*scalars, *arrays, *extra)


def wait(copies):
    for copy in copies:
        copy.wait()


def hot_columns(rows_ref, count_ref, g, nodes):
    rows = rows_ref[g : g + 1, :]
    lane = lax.broadcasted_iota(jnp.int32, rows.shape, 1)
    rows = jnp.where(lane < count_ref[0, g], rows, -1)
    node = lax.broadcasted_iota(jnp.int32, (nodes, rows.shape[1]), 0)
    return jnp.where(node == rows, 1.0, 0.0).astype(BF)


def pick_body(scalars, arrays, copies, outs):
    (count_ref,), (rows_ref, feat_ref), (out_ref,) = scalars, arrays, outs
    wait(copies)
    feat = feat_ref[...]
    for g in range(out_ref.shape[0]):
        hot = hot_columns(rows_ref, count_ref, g, feat.shape[0])
        out_ref[g] = lax.dot_general(hot, feat, TN, preferred_element_type=F32).astype(BF)


def spot_of(index_ref, t, k):
    index = index_ref[t, k]
    z, x = lax.shift_right_logical(index, 1) & (NZ - 1), lax.shift_right_logical(index, 4)
    return (z * NX + x) * 2 + (index & 1)


def main_body(scalars, arrays, copies, outs, tiles, acc, terms, tile_sem, term_sems):
    index_ref, count_ref = scalars
    blocks_ref, outer_ref, pre_ref, w_ref, dout_ref = arrays[:5]
    out_ref, dpre_ref, dagg_ref, agg_ref, term_ref = outs
    slots = blocks_ref.shape[1]
    spare = 2 * BANDS
    tiles[spare] = jnp.zeros(tiles.shape[1:], BF)

    def clear(i, carry):
        acc[i] = jnp.zeros(acc.shape[1:], F32)
        return carry

    lax.fori_loop(0, spare, clear, 0)
    wait(copies)
    for t in range(2):
        rows = pl.ds(t * 128, 128)
        spots = [
            jnp.where(k < count_ref[t], spot_of(index_ref, t, k), spare) for k in range(slots)
        ]
        total = outer_ref[rows, :]
        for k in range(0, slots, 2):
            left = jnp.concatenate([blocks_ref[t, k], blocks_ref[t, k + 1]], axis=1)
            right = jnp.concatenate([tiles[spots[k]], tiles[spots[k + 1]]], axis=0)
            total = total + jnp.dot(left, right, preferred_element_type=F32)
        agg = total.astype(BF)
        agg_ref[rows, :] = agg
        pre = pre_ref[rows, :] + jnp.dot(agg, w_ref[...], preferred_element_type=F32)
        sig = jax.nn.sigmoid(pre)
        out_ref[rows, :] = (pre * sig).astype(BF)
        d_pre = (dout_ref[rows, :].astype(F32) * sig * (1.0 + pre * (1.0 - sig))).astype(BF)
        dpre_ref[rows, :] = d_pre
        d_agg = lax.dot_general(d_pre, w_ref[...], NT, preferred_element_type=F32).astype(BF)
        dagg_ref[rows, :] = d_agg
        for k in range(slots):
            term = lax.dot_general(blocks_ref[t, k], d_agg, TN, preferred_element_type=F32)
            acc[spots[k]] = acc[spots[k]] + term
    stores = []
    for c in range(STORE):
        part = pl.ds(c * (spare // STORE), spare // STORE)

        def convert(i, carry):
            terms[i] = acc[i].astype(BF)
            return carry

        lax.fori_loop(part.start, part.start + part.size, convert, 0)
        store = pltpu.make_async_copy(terms.at[part], term_ref.at[part], term_sems.at[c])
        store.start()
        stores.append(store)
    wait(stores)


def main_kernel(scalars, arrays, gathered, outs):
    count = len(arrays)

    def kernel(*refs):
        scalar_refs, refs = refs[:2], refs[2:]
        sources, gathered_ref, refs = refs[:count], refs[count], refs[count + 1 :]
        outputs, refs = refs[: len(outs)], refs[len(outs) :]
        buffers, (sems, tiles, acc, terms, tile_sem, term_sems) = refs[:count], refs[count:]
        copies = [pltpu.make_async_copy(gathered_ref, tiles.at[pl.ds(0, 2 * BANDS)], tile_sem)] + [
            pltpu.make_async_copy(source, buffer, sems.at[i])
            for i, (source, buffer) in enumerate(zip(sources, buffers, strict=True))
        ]
        for copy in copies:
            copy.start()
        main_body(scalar_refs, buffers, copies, outputs, tiles, acc, terms, tile_sem, term_sems)

    shape = (2 * BANDS + 1, *gathered.shape[1:])
    return pl.pallas_call(
        kernel,
        out_shape=tuple(outs),
        in_specs=[SMEM] * 2 + [HBM] * (count + 1),
        out_specs=(VMEM,) * (len(outs) - 1) + (HBM,),
        scratch_shapes=[
            *(pltpu.VMEM(a.shape, a.dtype) for a in arrays),
            pltpu.SemaphoreType.DMA((count,)),
            pltpu.VMEM(shape, BF),
            pltpu.VMEM(shape, F32),
            pltpu.VMEM(gathered.shape, BF),
            pltpu.SemaphoreType.DMA,
            pltpu.SemaphoreType.DMA((STORE,)),
        ],
        compiler_params=pltpu.CompilerParams(vmem_limit_bytes=60 << 20),
        cost_estimate=pl.CostEstimate(flops=1 << 30, bytes_accessed=12 << 20, transcendentals=0),
    )(*scalars, *arrays, gathered)


def third_body(scalars, arrays, copies, outs):
    dpre_ref, agg_ref, feat_ref, w_ref = arrays
    part_ref, self_ref = outs
    wait(copies)
    d_pre = dpre_ref[...]
    width = d_pre.shape[1]
    groups, rows, _ = part_ref.shape
    share = 2 * width // groups
    for i, ref in enumerate((feat_ref, agg_ref)):
        grad = lax.dot_general(ref[...], d_pre, TN, preferred_element_type=F32).astype(BF)
        for g in range(groups // 2):
            part_ref[i * groups // 2 + g, pl.ds(0, share), :] = grad[g * share : (g + 1) * share]
    bias = jnp.sum(d_pre.astype(F32), axis=0, keepdims=True)
    rest = rows - share
    row = lax.broadcasted_iota(jnp.int32, (rest, width), 0)
    part_ref[0, pl.ds(share, rest), :] = jnp.where(row == 0, bias, 0.0).astype(BF)
    for g in range(1, groups):
        part_ref[g, pl.ds(share, rest), :] = jnp.zeros((rest, width), BF)
    self_ref[...] = lax.dot_general(d_pre, w_ref[...], NT, preferred_element_type=F32)


def back_body(scalars, arrays, copies, outs):
    (cut_ref, dagg_ref), (back_ref,) = arrays, outs
    wait(copies)
    d_agg = dagg_ref[...]
    cut = back_ref.shape[1]
    for g in range(0, back_ref.shape[0], 2):
        rows = lax.dot_general(
            cut_ref[:, pl.ds(g * cut, 2 * cut)], d_agg, TN, preferred_element_type=F32
        ).astype(BF)
        back_ref[g] = rows[:cut]
        back_ref[g + 1] = rows[cut:]


def blocks_body(scalars, arrays, copies, outs):
    (index_ref, count_ref), (tiles, dagg_ref), (out_ref,) = scalars, arrays, outs
    wait(copies)
    for t in range(2):
        d_agg = dagg_ref[pl.ds(t * 128, 128), :]
        for k in range(out_ref.shape[1]):
            live = jnp.where(k < count_ref[t], 1.0, 0.0)
            tile = tiles[spot_of(index_ref, t, k)]
            grad = lax.dot_general(d_agg, tile, NT, preferred_element_type=F32)
            out_ref[t, k] = (grad * live).astype(BF)


def base_body(scalars, arrays, copies, outs):
    (count_ref,), (rows_ref, back_ref, self_ref), (out_ref,) = scalars, arrays, outs
    wait(copies)
    total = self_ref[...]
    for g in range(0, back_ref.shape[0], 2):
        hot = jnp.concatenate(
            [hot_columns(rows_ref, count_ref, g + i, total.shape[0]) for i in range(2)], axis=1
        )
        rows = jnp.concatenate([back_ref[g], back_ref[g + 1]], axis=0)
        total = total + jnp.dot(hot, rows, preferred_element_type=F32)
    out_ref[...] = total


def sum_body(scalars, arrays, copies, outs):
    (parts_ref,), (out_ref,) = arrays, outs
    wait(copies)
    total = parts_ref[0].astype(F32)
    for i in range(1, parts_ref.shape[0]):
        total = total + parts_ref[i].astype(F32)
    for i in range(out_ref.shape[0]):
        out_ref[i] = total.astype(BF)


def a2a(x, axis):
    return lax.all_to_all(x, axis, 0, 0, tiled=True)


def shift(x, axis, n, by):
    return lax.ppermute(x, axis, [(i, (i + by) % n) for i in range(n)])


def local(
    features, block_index, block_count, block_values, cut_weight, send_rows, send_count,
    w_self, w_neigh, bias, d_out,
):
    nodes, width = features.shape
    tiles_here, slots = block_index.shape
    scale = 1.0 / math.sqrt(nodes * NG * BANDS)
    rows2 = send_rows.reshape(NG, -1)
    cut = rows2.shape[1]
    node_bf, node_f32 = sds((nodes, width), BF), sds((nodes, width), F32)
    cut_bf = sds((NG, cut, width), BF)

    gathered = lax.all_gather(features, "x", axis=0, tiled=True)
    gathered = lax.all_gather(gathered, "z", axis=0, tiled=True).reshape(2 * BANDS, 128, width)

    (outgoing,) = call(
        pick_body, [send_count], [rows2, features], [cut_bf], flops=2 * NG * cut * width * nodes
    )
    arrived = a2a(outgoing, ("y", "c")).reshape(NG * cut, width)
    outer = jnp.dot(cut_weight, arrived, preferred_element_type=F32)
    own_pre = jnp.dot(features, w_self, preferred_element_type=F32) + bias

    output, d_pre, d_agg, aggregate, terms = main_kernel(
        [block_index, block_count],
        [block_values, outer, own_pre, w_neigh, d_out],
        gathered,
        [node_bf, node_bf, node_bf, node_bf, sds(gathered.shape, BF)],
    )

    terms = lax.psum_scatter(terms.reshape(NZ, NX * nodes, width), "z", scatter_dimension=0)
    terms = terms.reshape(NX, nodes, width)
    me = lax.axis_index("x")
    own_back = lax.dynamic_index_in_dim(terms, me, 0, keepdims=False).astype(F32)
    for by in range(1, NX):
        away = lax.dynamic_index_in_dim(terms, (me + by) & (NX - 1), 0, keepdims=False)
        own_back = own_back + shift(away, "x", NX, by).astype(F32)

    part, self_back = call(
        third_body, [], [d_pre, aggregate, features, w_self],
        [sds((NG, GRAD_ROWS, width), BF), node_f32], flops=100 << 20,
    )
    part = jnp.sum(a2a(part, ("y", "c")).astype(F32), axis=0).astype(BF)
    (back,) = call(
        back_body, [], [cut_weight, d_agg], [cut_bf], extra=[part],
        flops=2 * NG * cut * width * nodes,
    )
    returned = a2a(back, ("y", "c"))
    part = jnp.sum(lax.all_gather(part, "x", axis=0).astype(F32), axis=0).astype(BF)
    part = lax.all_gather(part, "z", axis=0)
    (part,) = call(sum_body, [], [part], [sds((NY, GRAD_ROWS, width), BF)], extra=[returned])
    part = a2a(part, "y")
    grads = lax.all_gather(part, "c", axis=1).reshape(NG, GRAD_ROWS, width)
    grads = grads.astype(F32) * scale
    share = 2 * width // NG
    weight_grads = grads[:, :share].reshape(2, width, width)
    (base,) = call(
        base_body, [send_count], [rows2, returned, self_back], [node_f32],
        flops=2 * NG * cut * width * nodes,
    )
    d_features = (base + own_back).astype(BF)

    (grad_blocks,) = call(
        blocks_body, [block_index, block_count], [gathered, d_agg], [sds(block_values.shape, BF)],
        extra=[grads], flops=2 * tiles_here * slots * 128 * 128 * width,
    )

    return (
        output,
        d_features,
        grad_blocks,
        weight_grads[0],
        weight_grads[1],
        grads[0, share],
    )


def solution(mesh):
    mesh = Mesh(mesh.devices.reshape(NY, NC, NX, NZ), ("y", "c", "x", "z"))
    rows = ("y", "c", "x", "z")
    split = [P(rows)] * 7 + [P()] * 3 + [P(rows)]
    return jax.shard_map(
        local,
        mesh=mesh,
        in_specs=tuple(split),
        out_specs=(P(rows), P(rows), P(rows), P(), P(), P()),
        check_vma=False,
    )
```

```python
import math

import jax
import jax.numpy as jnp
from jax import lax
from jax.experimental import pallas as pl
from jax.experimental.pallas import tpu as pltpu
from jax.sharding import Mesh, PartitionSpec as P

BF = jnp.bfloat16
F32 = jnp.float32
TN = (((0,), (0,)), ((), ()))
NT = (((1,), (1,)), ((), ()))
NX, NZ, NY, NC = 4, 8, 8, 2
NG = NY * NC
BANDS = NX * NZ
GRAD_ROWS = 48
STORE = 8
VMEM = pl.BlockSpec(memory_space=pltpu.VMEM)
SMEM = pl.BlockSpec(memory_space=pltpu.SMEM)
HBM = pl.BlockSpec(memory_space=pltpu.HBM)


def sds(shape, dtype):
    return jax.ShapeDtypeStruct(shape, dtype)


def call(
    body, scalars, arrays, outs, out_specs=None, scratch=(), direct=(), extra=(), flops=0, vmem=60
):
    count, first = len(arrays), len(scalars)

    def kernel(*refs):
        sources = refs[first : first + count]
        rest = refs[first + count :]
        given, rest = rest[: len(direct)], rest[len(direct) + len(extra) :]
        outputs, rest = rest[: len(outs)], rest[len(outs) :]
        buffers, sems, rest = rest[:count], rest[count], rest[count + 1 :]
        copies = [
            pltpu.make_async_copy(source, buffer, sems.at[i])
            for i, (source, buffer) in enumerate(zip(sources, buffers, strict=True))
        ]
        for copy in copies:
            copy.start()
        body(refs[:first], buffers, copies, outputs, *([given] if direct else []), *rest)

    nbytes = sum(a.size * a.dtype.itemsize for a in (*arrays, *outs, *direct))
    return pl.pallas_call(
        kernel,
        out_shape=tuple(outs),
        in_specs=[SMEM] * first + [HBM] * (count + len(direct) + len(extra)),
        out_specs=tuple(out_specs or [VMEM] * len(outs)),
        scratch_shapes=[
            *(pltpu.VMEM(a.shape, a.dtype) for a in arrays),
            pltpu.SemaphoreType.DMA((count,)),
            *scratch,
        ],
        compiler_params=pltpu.CompilerParams(vmem_limit_bytes=vmem << 20),
        cost_estimate=pl.CostEstimate(flops=flops, bytes_accessed=nbytes, transcendentals=0),
    )(*scalars, *arrays, *direct, *extra)


def wait(copies):
    for copy in copies:
        copy.wait()


def hot_columns(rows_ref, count_ref, g, nodes):
    rows = rows_ref[g : g + 1, :]
    lane = lax.broadcasted_iota(jnp.int32, rows.shape, 1)
    rows = jnp.where(lane < count_ref[0, g], rows, -1)
    node = lax.broadcasted_iota(jnp.int32, (nodes, rows.shape[1]), 0)
    return jnp.where(node == rows, 1.0, 0.0).astype(BF)


def pick_body(scalars, arrays, copies, outs):
    (count_ref,), (rows_ref, feat_ref), (out_ref,) = scalars, arrays, outs
    wait(copies)
    feat = feat_ref[...]
    for g in range(out_ref.shape[0]):
        hot = hot_columns(rows_ref, count_ref, g, feat.shape[0])
        out_ref[g] = lax.dot_general(hot, feat, TN, preferred_element_type=F32).astype(BF)


def band_of(index_ref, t, k):
    index = index_ref[t, k]
    return lax.shift_right_logical(index, 4), lax.shift_right_logical(index, 1) & (NZ - 1), index & 1


def tile_spot(index_ref, x_ref, t, k):
    x, z, odd = band_of(index_ref, t, k)
    even_spot = z * NX + ((x_ref[0] - x) & (NX - 1))
    odd_spot = BANDS + ((x - x_ref[0]) & (NX - 1)) * NZ + z
    return jnp.where(odd == 0, even_spot, odd_spot)


def term_spot(index_ref, t, k):
    x, z, odd = band_of(index_ref, t, k)
    return (z * NX + x) * 2 + odd


def fetch_tiles(sources, tiles, sems):
    starts = (0, BANDS, BANDS + NZ, BANDS + 2 * NZ, BANDS + 2 * NZ + NZ // 2, BANDS + 3 * NZ)
    copies = [
        pltpu.make_async_copy(source, tiles.at[pl.ds(start, source.shape[0])], sems.at[i])
        for i, (source, start) in enumerate(zip(sources, starts, strict=True))
    ]
    for copy in copies:
        copy.start()
    return copies


def forward_body(scalars, arrays, copies, outs, sources, tiles, tile_sems):
    index_ref, count_ref, x_ref = scalars
    blocks_ref, outer_ref, pre_ref, w_ref, dout_ref, feat_ref, wself_ref, cut_ref = arrays
    out_ref, dagg_ref, back_ref, self_ref = outs
    tile_copies = fetch_tiles(sources, tiles, tile_sems)
    slots = blocks_ref.shape[1]
    spare = 2 * BANDS
    tiles[spare] = jnp.zeros(tiles.shape[1:], BF)
    wait(copies)
    wait(tile_copies)
    aggs, d_pres, d_aggs = [], [], []
    for t in range(2):
        rows = pl.ds(t * 128, 128)
        spots = [
            jnp.where(k < count_ref[t], tile_spot(index_ref, x_ref, t, k), spare)
            for k in range(slots)
        ]
        total = outer_ref[rows, :]
        for k in range(0, slots, 2):
            left = jnp.concatenate([blocks_ref[t, k], blocks_ref[t, k + 1]], axis=1)
            right = jnp.concatenate([tiles[spots[k]], tiles[spots[k + 1]]], axis=0)
            total = total + jnp.dot(left, right, preferred_element_type=F32)
        agg = total.astype(BF)
        pre = pre_ref[rows, :] + jnp.dot(agg, w_ref[...], preferred_element_type=F32)
        sig = jax.nn.sigmoid(pre)
        out_ref[rows, :] = (pre * sig).astype(BF)
        d_pre = (dout_ref[rows, :].astype(F32) * sig * (1.0 + pre * (1.0 - sig))).astype(BF)
        d_agg = lax.dot_general(d_pre, w_ref[...], NT, preferred_element_type=F32).astype(BF)
        dagg_ref[rows, :] = d_agg
        d_aggs.append(d_agg)
        aggs.append(agg)
        d_pres.append(d_pre)
    agg, d_pre = jnp.concatenate(aggs, axis=0), jnp.concatenate(d_pres, axis=0)
    width = d_pre.shape[1]
    groups = back_ref.shape[0]
    cut = cut_ref.shape[1] // groups
    share = 2 * width // groups
    rest = back_ref.shape[1] - cut - share
    for i, left in enumerate((feat_ref[...], agg)):
        grad = lax.dot_general(left, d_pre, TN, preferred_element_type=F32).astype(BF)
        for g in range(groups // 2):
            spot = i * groups // 2 + g
            back_ref[spot, pl.ds(cut, share), :] = grad[g * share : (g + 1) * share]
    bias = jnp.sum(d_pre.astype(F32), axis=0, keepdims=True)
    row = lax.broadcasted_iota(jnp.int32, (rest, width), 0)
    back_ref[0, pl.ds(cut + share, rest), :] = jnp.where(row == 0, bias, 0.0).astype(BF)
    for g in range(1, groups):
        back_ref[g, pl.ds(cut + share, rest), :] = jnp.zeros((rest, width), BF)
    d_agg = jnp.concatenate(d_aggs, axis=0)
    for g in range(0, groups, 2):
        rows = lax.dot_general(
            cut_ref[:, pl.ds(g * cut, 2 * cut)], d_agg, TN, preferred_element_type=F32
        ).astype(BF)
        back_ref[g, pl.ds(0, cut), :] = rows[:cut]
        back_ref[g + 1, pl.ds(0, cut), :] = rows[cut:]
    self_ref[...] = lax.dot_general(d_pre, wself_ref[...], NT, preferred_element_type=F32)


def terms_body(scalars, arrays, copies, outs, acc, terms, sems):
    (index_ref, count_ref), (blocks_ref, dagg_ref), (term_ref,) = scalars, arrays, outs
    slots = blocks_ref.shape[1]
    spare = 2 * BANDS

    def clear(i, carry):
        acc[i] = jnp.zeros(acc.shape[1:], F32)
        return carry

    lax.fori_loop(0, spare, clear, 0)
    wait(copies)
    for t in range(2):
        d_agg = dagg_ref[pl.ds(t * 128, 128), :]
        for k in range(slots):
            spot = jnp.where(k < count_ref[t], term_spot(index_ref, t, k), spare)
            term = lax.dot_general(blocks_ref[t, k], d_agg, TN, preferred_element_type=F32)
            acc[spot] = acc[spot] + term
    stores = []
    for c in range(STORE):
        part = pl.ds(c * (spare // STORE), spare // STORE)

        def convert(i, carry):
            terms[i] = acc[i].astype(BF)
            return carry

        lax.fori_loop(part.start, part.start + part.size, convert, 0)
        store = pltpu.make_async_copy(terms.at[part], term_ref.at[part], sems.at[c])
        store.start()
        stores.append(store)
    wait(stores)


def blocks_body(scalars, arrays, copies, outs, sources, tiles, tile_sems):
    (index_ref, count_ref, x_ref), (dagg_ref,), (out_ref,) = scalars, arrays, outs
    tile_copies = fetch_tiles(sources, tiles, tile_sems)
    wait(copies)
    wait(tile_copies)
    for t in range(2):
        d_agg = dagg_ref[pl.ds(t * 128, 128), :]
        for k in range(out_ref.shape[1]):
            live = jnp.where(k < count_ref[t], 1.0, 0.0)
            tile = tiles[tile_spot(index_ref, x_ref, t, k)]
            grad = lax.dot_general(d_agg, tile, NT, preferred_element_type=F32)
            out_ref[t, k] = (grad * live).astype(BF)


def base_body(scalars, arrays, copies, outs):
    (count_ref,), (rows_ref, back_ref, self_ref), (out_ref,) = scalars, arrays, outs
    cut = rows_ref.shape[1]
    wait(copies)
    total = self_ref[...]
    for g in range(0, back_ref.shape[0], 2):
        hot = jnp.concatenate(
            [hot_columns(rows_ref, count_ref, g + i, total.shape[0]) for i in range(2)], axis=1
        )
        rows = jnp.concatenate([back_ref[g + i, pl.ds(0, cut), :] for i in range(2)], axis=0)
        total = total + jnp.dot(hot, rows, preferred_element_type=F32)
    out_ref[...] = total


def sum_body(scalars, arrays, copies, outs):
    (parts_ref,), (out_ref,) = arrays, outs
    wait(copies)
    total = parts_ref[0].astype(F32)
    for i in range(1, parts_ref.shape[0]):
        total = total + parts_ref[i].astype(F32)
    for i in range(out_ref.shape[0]):
        out_ref[i] = total.astype(BF)


def a2a(x, axis):
    return lax.all_to_all(x, axis, 0, 0, tiled=True)


def shift(x, axis, n, by):
    return lax.ppermute(x, axis, [(i, (i + by) % n) for i in range(n)])


def local(
    features, block_index, block_count, block_values, cut_weight, send_rows, send_count,
    w_self, w_neigh, bias, d_out,
):
    nodes, width = features.shape
    tiles_here, slots = block_index.shape
    scale = 1.0 / math.sqrt(nodes * NG * BANDS)
    rows2 = send_rows.reshape(NG, -1)
    cut = rows2.shape[1]
    node_bf, node_f32 = sds((nodes, width), BF), sds((nodes, width), F32)
    cut_bf = sds((NG, cut, width), BF)

    even, odd = features[:128], features[128:]
    own = a2a(jnp.broadcast_to(odd[None], (NZ, *odd.shape)), "z")
    even = jnp.stack([even] + [shift(even, "x", NX, by) for by in range(1, NX)])
    even = lax.all_gather(even, "z", axis=0, tiled=True)
    left, right = shift(own, "x", NX, 1), shift(own, "x", NX, -1)
    far_low = shift(left[: NZ // 2], "x", NX, 1)
    far_high = shift(right[NZ // 2 :], "x", NX, -1)
    gathered = (even, own, right, far_low, far_high, left)
    me = lax.axis_index("x")
    my_x = me.astype(jnp.int32).reshape(1)

    (outgoing,) = call(
        pick_body, [send_count], [rows2, features], [cut_bf], flops=2 * NG * cut * width * nodes,
    )
    arrived = a2a(outgoing, ("y", "c")).reshape(NG * cut, width)
    outer = jnp.dot(cut_weight, arrived, preferred_element_type=F32)
    own_pre = jnp.dot(features, w_self, preferred_element_type=F32) + bias

    tiles = pltpu.VMEM((2 * BANDS + 1, 128, width), BF)
    output, d_agg, back, self_back = call(
        forward_body,
        [block_index, block_count, my_x],
        [block_values, outer, own_pre, w_neigh, d_out, features, w_self, cut_weight],
        [node_bf, node_bf, sds((NG, cut + GRAD_ROWS, width), BF), node_f32],
        scratch=[tiles, pltpu.SemaphoreType.DMA((6,))],
        direct=gathered,
        flops=1 << 29,
    )
    (terms,) = call(
        terms_body,
        [block_index, block_count],
        [block_values, d_agg],
        [sds((2 * BANDS, 128, width), BF)],
        out_specs=[HBM],
        scratch=[
            pltpu.VMEM((2 * BANDS + 1, 128, width), F32),
            pltpu.VMEM((2 * BANDS, 128, width), BF),
            pltpu.SemaphoreType.DMA((STORE,)),
        ],
        flops=1 << 29,
    )

    terms = lax.psum_scatter(terms.reshape(NZ, NX * nodes, width), "z", scatter_dimension=0)
    terms = terms.reshape(NX, nodes, width)
    own_back = lax.dynamic_index_in_dim(terms, me, 0, keepdims=False).astype(F32)
    for by in range(1, NX):
        away = lax.dynamic_index_in_dim(terms, (me + by) & (NX - 1), 0, keepdims=False)
        own_back = own_back + shift(away, "x", NX, by).astype(F32)

    returned = a2a(back, ("y", "c"))
    part = jnp.sum(returned[:, cut:].astype(F32), axis=0).astype(BF)
    part = a2a(jnp.broadcast_to(part[None], (NX, *part.shape)), "x")
    part = jnp.sum(part.astype(F32), axis=0).astype(BF)
    part = a2a(jnp.broadcast_to(part[None], (NZ, *part.shape)), "z")
    (part,) = call(sum_body, [], [part], [sds((NY, GRAD_ROWS, width), BF)], extra=[terms])
    part = a2a(part, "y")
    grads = lax.all_gather(part, "c", axis=1).reshape(NG, GRAD_ROWS, width)
    grads = grads.astype(F32) * scale
    share = 2 * width // NG
    weight_grads = grads[:, :share].reshape(2, width, width)

    (grad_blocks,) = call(
        blocks_body, [block_index, block_count, my_x], [d_agg], [sds(block_values.shape, BF)],
        scratch=[tiles, pltpu.SemaphoreType.DMA((6,))], direct=gathered,
        flops=2 * tiles_here * slots * 128 * 128 * width,
    )
    (base,) = call(
        base_body, [send_count], [rows2, returned, self_back], [node_f32],
        flops=2 * NG * cut * width * nodes,
    )
    d_features = (base + own_back).astype(BF)

    return (
        output,
        d_features,
        grad_blocks,
        weight_grads[0],
        weight_grads[1],
        grads[0, share],
    )


def solution(mesh):
    mesh = Mesh(mesh.devices.reshape(NY, NC, NX, NZ), ("y", "c", "x", "z"))
    rows = ("y", "c", "x", "z")
    split = [P(rows)] * 7 + [P()] * 3 + [P(rows)]
    return jax.shard_map(
        local,
        mesh=mesh,
        in_specs=tuple(split),
        out_specs=(P(rows), P(rows), P(rows), P(), P(), P()),
        check_vma=False,
    )
```

```python
import math

import jax
import jax.numpy as jnp
from jax import lax
from jax.experimental import pallas as pl
from jax.experimental.pallas import tpu as pltpu
from jax.sharding import Mesh, PartitionSpec as P

BF = jnp.bfloat16
F32 = jnp.float32
TN = (((0,), (0,)), ((), ()))
NT = (((1,), (1,)), ((), ()))
NX, NZ, NY, NC = 4, 8, 8, 2
NG = NY * NC
BANDS = NX * NZ
SPARE_ROWS = 16
STORE = 8
VMEM = pl.BlockSpec(memory_space=pltpu.VMEM)
SMEM = pl.BlockSpec(memory_space=pltpu.SMEM)
HBM = pl.BlockSpec(memory_space=pltpu.HBM)


def sds(shape, dtype):
    return jax.ShapeDtypeStruct(shape, dtype)


def call(
    body, scalars, arrays, outs, out_specs=None, scratch=(), direct=(), extra=(), flops=0, vmem=60
):
    count, first = len(arrays), len(scalars)

    def kernel(*refs):
        sources = refs[first : first + count]
        rest = refs[first + count :]
        given, rest = rest[: len(direct)], rest[len(direct) + len(extra) :]
        outputs, rest = rest[: len(outs)], rest[len(outs) :]
        buffers, sems, rest = rest[:count], rest[count], rest[count + 1 :]
        copies = [
            pltpu.make_async_copy(source, buffer, sems.at[i])
            for i, (source, buffer) in enumerate(zip(sources, buffers, strict=True))
        ]
        for copy in copies:
            copy.start()
        body(refs[:first], buffers, copies, outputs, *([given] if direct else []), *rest)

    nbytes = sum(a.size * a.dtype.itemsize for a in (*arrays, *outs, *direct))
    return pl.pallas_call(
        kernel,
        out_shape=tuple(outs),
        in_specs=[SMEM] * first + [HBM] * (count + len(direct) + len(extra)),
        out_specs=tuple(out_specs or [VMEM] * len(outs)),
        scratch_shapes=[
            *(pltpu.VMEM(a.shape, a.dtype) for a in arrays),
            pltpu.SemaphoreType.DMA((count,)),
            *scratch,
        ],
        compiler_params=pltpu.CompilerParams(vmem_limit_bytes=vmem << 20),
        cost_estimate=pl.CostEstimate(flops=flops, bytes_accessed=nbytes, transcendentals=0),
    )(*scalars, *arrays, *direct, *extra)


def wait(copies):
    for copy in copies:
        copy.wait()


def hot_columns(rows_ref, count_ref, g, nodes):
    rows = rows_ref[g : g + 1, :]
    lane = lax.broadcasted_iota(jnp.int32, rows.shape, 1)
    rows = jnp.where(lane < count_ref[0, g], rows, -1)
    node = lax.broadcasted_iota(jnp.int32, (nodes, rows.shape[1]), 0)
    return jnp.where(node == rows, 1.0, 0.0).astype(BF)


def pick_body(scalars, arrays, copies, outs):
    (count_ref,), (rows_ref, feat_ref), (out_ref,) = scalars, arrays, outs
    wait(copies)
    feat = feat_ref[...]
    for g in range(out_ref.shape[0]):
        hot = hot_columns(rows_ref, count_ref, g, feat.shape[0])
        out_ref[g] = lax.dot_general(hot, feat, TN, preferred_element_type=F32).astype(BF)


def spot_of(index_ref, t, k):
    index = index_ref[t, k]
    z, x = lax.shift_right_logical(index, 1) & (NZ - 1), lax.shift_right_logical(index, 4)
    return (z * NX + x) * 2 + (index & 1)


def forward_body(scalars, arrays, copies, outs, gathered, tiles, tile_sem):
    index_ref, count_ref = scalars
    blocks_ref, outer_ref, pre_ref, w_ref, dout_ref, feat_ref, wself_ref, cut_ref = arrays
    out_ref, dagg_ref, back_ref, part_ref, self_ref = outs
    tile_copy = pltpu.make_async_copy(gathered[0], tiles.at[pl.ds(0, 2 * BANDS)], tile_sem)
    tile_copy.start()
    slots = blocks_ref.shape[1]
    spare = 2 * BANDS
    tiles[spare] = jnp.zeros(tiles.shape[1:], BF)
    wait(copies)
    tile_copy.wait()
    aggs, d_pres, d_aggs = [], [], []
    for t in range(2):
        rows = pl.ds(t * 128, 128)
        spots = [
            jnp.where(k < count_ref[t], spot_of(index_ref, t, k), spare)
            for k in range(slots)
        ]
        total = outer_ref[rows, :]
        for k in range(0, slots, 2):
            left = jnp.concatenate([blocks_ref[t, k], blocks_ref[t, k + 1]], axis=1)
            right = jnp.concatenate([tiles[spots[k]], tiles[spots[k + 1]]], axis=0)
            total = total + jnp.dot(left, right, preferred_element_type=F32)
        agg = total.astype(BF)
        pre = pre_ref[rows, :] + jnp.dot(agg, w_ref[...], preferred_element_type=F32)
        sig = jax.nn.sigmoid(pre)
        out_ref[rows, :] = (pre * sig).astype(BF)
        d_pre = (dout_ref[rows, :].astype(F32) * sig * (1.0 + pre * (1.0 - sig))).astype(BF)
        d_agg = lax.dot_general(d_pre, w_ref[...], NT, preferred_element_type=F32).astype(BF)
        dagg_ref[rows, :] = d_agg
        d_aggs.append(d_agg)
        aggs.append(agg)
        d_pres.append(d_pre)
    agg, d_pre = jnp.concatenate(aggs, axis=0), jnp.concatenate(d_pres, axis=0)
    width = d_pre.shape[1]
    groups = back_ref.shape[0]
    cut = cut_ref.shape[1] // groups
    share = part_ref.shape[1] - SPARE_ROWS
    grads = [
        lax.dot_general(left, d_pre, TN, preferred_element_type=F32).astype(BF)
        for left in (feat_ref[...], agg)
    ]
    bias = jnp.sum(d_pre.astype(F32), axis=0, keepdims=True)
    row = lax.broadcasted_iota(jnp.int32, (SPARE_ROWS, width), 0)
    bias = jnp.where(row == 0, bias, 0.0).astype(BF)
    for x in range(NX):
        grad, at = grads[2 * x // NX], x % 2 * share
        part_ref[x, pl.ds(0, share), :] = grad[at : at + share]
        part_ref[x, pl.ds(share, SPARE_ROWS), :] = bias
    d_agg = jnp.concatenate(d_aggs, axis=0)
    for g in range(0, groups, 2):
        rows = lax.dot_general(
            cut_ref[:, pl.ds(g * cut, 2 * cut)], d_agg, TN, preferred_element_type=F32
        ).astype(BF)
        back_ref[g, pl.ds(0, cut), :] = rows[:cut]
        back_ref[g + 1, pl.ds(0, cut), :] = rows[cut:]
    self_ref[...] = lax.dot_general(d_pre, wself_ref[...], NT, preferred_element_type=F32)


def terms_body(scalars, arrays, copies, outs, acc, terms, sems):
    (index_ref, count_ref), (blocks_ref, dagg_ref), (term_ref,) = scalars, arrays, outs
    slots = blocks_ref.shape[1]
    spare = 2 * BANDS

    def clear(i, carry):
        acc[i] = jnp.zeros(acc.shape[1:], F32)
        return carry

    lax.fori_loop(0, spare, clear, 0)
    wait(copies)
    for t in range(2):
        d_agg = dagg_ref[pl.ds(t * 128, 128), :]
        for k in range(slots):
            spot = jnp.where(k < count_ref[t], spot_of(index_ref, t, k), spare)
            term = lax.dot_general(blocks_ref[t, k], d_agg, TN, preferred_element_type=F32)
            acc[spot] = acc[spot] + term
    stores = []
    for c in range(STORE):
        part = pl.ds(c * (spare // STORE), spare // STORE)

        def convert(i, carry):
            terms[i] = acc[i].astype(BF)
            return carry

        lax.fori_loop(part.start, part.start + part.size, convert, 0)
        store = pltpu.make_async_copy(terms.at[part], term_ref.at[part], sems.at[c])
        store.start()
        stores.append(store)
    wait(stores)


def blocks_body(scalars, arrays, copies, outs):
    (index_ref, count_ref), (dagg_ref, tiles), (out_ref,) = scalars, arrays, outs
    wait(copies)
    for t in range(2):
        d_agg = dagg_ref[pl.ds(t * 128, 128), :]
        for k in range(out_ref.shape[1]):
            live = jnp.where(k < count_ref[t], 1.0, 0.0)
            tile = tiles[spot_of(index_ref, t, k)]
            grad = lax.dot_general(d_agg, tile, NT, preferred_element_type=F32)
            out_ref[t, k] = (grad * live).astype(BF)


def base_body(scalars, arrays, copies, outs):
    (count_ref,), (rows_ref, back_ref, self_ref, *term_refs), (out_ref,) = scalars, arrays, outs
    wait(copies)
    total = self_ref[...]
    for term_ref in term_refs:
        total = total + term_ref[...].astype(F32)
    for g in range(0, back_ref.shape[0], 2):
        hot = jnp.concatenate(
            [hot_columns(rows_ref, count_ref, g + i, total.shape[0]) for i in range(2)], axis=1
        )
        rows = jnp.concatenate([back_ref[g], back_ref[g + 1]], axis=0)
        total = total + jnp.dot(hot, rows, preferred_element_type=F32)
    out_ref[...] = total.astype(BF)


def share_body(scalars, arrays, copies, outs):
    (parts_ref,), (out_ref,) = arrays, outs
    wait(copies)
    total = parts_ref[0].astype(F32)
    for i in range(1, parts_ref.shape[0]):
        total = total + parts_ref[i].astype(F32)
    total = total.astype(BF)
    share = out_ref.shape[1] - SPARE_ROWS
    last = total.shape[0] - SPARE_ROWS
    for i in range(out_ref.shape[0]):
        out_ref[i, pl.ds(0, share), :] = total[i * share : (i + 1) * share]
        out_ref[i, pl.ds(share, SPARE_ROWS), :] = total[last:]


def gate(x, after):
    return pl.pallas_call(
        lambda x_ref, after_ref, out_ref: None,
        out_shape=sds(x.shape, x.dtype),
        in_specs=[HBM, HBM],
        out_specs=HBM,
        input_output_aliases={0: 0},
        compiler_params=pltpu.CompilerParams(vmem_limit_bytes=60 << 20),
    )(x, after)


def a2a(x, axis):
    return lax.all_to_all(x, axis, 0, 0, tiled=True)


def shift(x, axis, n, by):
    return lax.ppermute(x, axis, [(i, (i + by) % n) for i in range(n)])


def local(
    features, block_index, block_count, block_values, cut_weight, send_rows, send_count,
    w_self, w_neigh, bias, d_out,
):
    nodes, width = features.shape
    tiles_here, slots = block_index.shape
    scale = 1.0 / math.sqrt(nodes * NG * BANDS)
    rows2 = send_rows.reshape(NG, -1)
    cut = rows2.shape[1]
    node_bf, node_f32 = sds((nodes, width), BF), sds((nodes, width), F32)
    cut_bf = sds((NG, cut, width), BF)

    gathered = lax.all_gather(features, "x", axis=0, tiled=True)
    gathered = lax.all_gather(gathered, "z", axis=0, tiled=True).reshape(2 * BANDS, 128, width)

    (outgoing,) = call(
        pick_body, [send_count], [rows2, features], [cut_bf], flops=2 * NG * cut * width * nodes,
    )
    arrived = a2a(outgoing, ("y", "c")).reshape(NG * cut, width)
    outer = jnp.dot(cut_weight, arrived, preferred_element_type=F32)
    own_pre = jnp.dot(features, w_self, preferred_element_type=F32) + bias

    output, d_agg, back, part, self_back = call(
        forward_body,
        [block_index, block_count],
        [block_values, outer, own_pre, w_neigh, d_out, features, w_self, cut_weight],
        [node_bf, node_bf, cut_bf, sds((NX, 2 * width // NX + SPARE_ROWS, width), BF), node_f32],
        scratch=[pltpu.VMEM((2 * BANDS + 1, 128, width), BF), pltpu.SemaphoreType.DMA],
        direct=[gathered],
        flops=1 << 29,
    )
    (terms,) = call(
        terms_body,
        [block_index, block_count],
        [block_values, d_agg],
        [sds((2 * BANDS, 128, width), BF)],
        out_specs=[HBM],
        scratch=[
            pltpu.VMEM((2 * BANDS + 1, 128, width), F32),
            pltpu.VMEM((2 * BANDS, 128, width), BF),
            pltpu.SemaphoreType.DMA((STORE,)),
        ],
        flops=1 << 29,
    )

    terms = lax.psum_scatter(terms.reshape(NZ, NX * nodes, width), "z", scatter_dimension=0)
    terms = terms.reshape(NX, nodes, width)
    me = lax.axis_index("x")
    own_terms = [lax.dynamic_index_in_dim(terms, me, 0, keepdims=False)]
    for by in range(1, NX):
        away = lax.dynamic_index_in_dim(terms, (me + by) & (NX - 1), 0, keepdims=False)
        own_terms.append(shift(away, "x", NX, by))

    part = a2a(part, "x")
    (part,) = call(
        share_body, [], [part], [sds((NZ, 2 * width // BANDS + SPARE_ROWS, width), BF)]
    )
    part = jnp.sum(a2a(part, "z").astype(F32), axis=0).astype(BF)
    part = a2a(jnp.broadcast_to(part[None], (NG, *part.shape)), ("y", "c"))
    part = jnp.sum(part.astype(F32), axis=0).astype(BF)
    returned = a2a(gate(back, part), ("y", "c"))
    part = gate(lax.all_gather(part, "x", axis=0), terms)
    part = lax.all_gather(part, "z", axis=1).astype(F32) * scale
    share = 2 * width // BANDS
    weight_grads = part[:, :, :share].reshape(2, width, width)

    (grad_blocks,) = call(
        blocks_body, [block_index, block_count], [d_agg, gathered], [sds(block_values.shape, BF)],
        flops=2 * tiles_here * slots * 128 * 128 * width,
    )
    (d_features,) = call(
        base_body, [send_count], [rows2, returned, self_back, *own_terms], [node_bf],
        flops=2 * NG * cut * width * nodes,
    )

    return (
        output,
        d_features,
        grad_blocks,
        weight_grads[0],
        weight_grads[1],
        part[0, 0, share],
    )


def solution(mesh):
    mesh = Mesh(mesh.devices.reshape(NY, NC, NX, NZ), ("y", "c", "x", "z"))
    rows = ("y", "c", "x", "z")
    split = [P(rows)] * 7 + [P()] * 3 + [P(rows)]
    return jax.shard_map(
        local,
        mesh=mesh,
        in_specs=tuple(split),
        out_specs=(P(rows), P(rows), P(rows), P(), P(), P()),
        check_vma=False,
    )
```

```python
import functools
import math

import jax
import jax.numpy as jnp
from jax import lax
from jax.experimental import pallas as pl
from jax.experimental.pallas import tpu as pltpu
from jax.sharding import Mesh, PartitionSpec as P

BF = jnp.bfloat16
F32 = jnp.float32
TN = (((0,), (0,)), ((), ()))
NT = (((1,), (1,)), ((), ()))
NX, NZ, NY, NC = 4, 8, 8, 2
NG = NY * NC
BANDS = NX * NZ
SPARE_ROWS = 16
STORE = 8
VMEM = pl.BlockSpec(memory_space=pltpu.VMEM)
SMEM = pl.BlockSpec(memory_space=pltpu.SMEM)
HBM = pl.BlockSpec(memory_space=pltpu.HBM)


def sds(shape, dtype):
    return jax.ShapeDtypeStruct(shape, dtype)


def call(
    body, scalars, arrays, outs, out_specs=None, scratch=(), direct=(), extra=(), flops=0, vmem=60
):
    count, first = len(arrays), len(scalars)

    def kernel(*refs):
        sources = refs[first : first + count]
        rest = refs[first + count :]
        given, rest = rest[: len(direct)], rest[len(direct) + len(extra) :]
        outputs, rest = rest[: len(outs)], rest[len(outs) :]
        buffers, sems, rest = rest[:count], rest[count], rest[count + 1 :]
        copies = [
            pltpu.make_async_copy(source, buffer, sems.at[i])
            for i, (source, buffer) in enumerate(zip(sources, buffers, strict=True))
        ]
        for copy in copies:
            copy.start()
        body(refs[:first], buffers, copies, outputs, *([given] if direct else []), *rest)

    nbytes = sum(a.size * a.dtype.itemsize for a in (*arrays, *outs, *direct))
    return pl.pallas_call(
        kernel,
        out_shape=tuple(outs),
        in_specs=[SMEM] * first + [HBM] * (count + len(direct) + len(extra)),
        out_specs=tuple(out_specs or [VMEM] * len(outs)),
        scratch_shapes=[
            *(pltpu.VMEM(a.shape, a.dtype) for a in arrays),
            pltpu.SemaphoreType.DMA((count,)),
            *scratch,
        ],
        compiler_params=pltpu.CompilerParams(vmem_limit_bytes=vmem << 20),
        cost_estimate=pl.CostEstimate(flops=flops, bytes_accessed=nbytes, transcendentals=0),
    )(*scalars, *arrays, *direct, *extra)


def wait(copies):
    for copy in copies:
        copy.wait()


def hot_columns(rows_ref, count_ref, g, nodes):
    rows = rows_ref[g : g + 1, :]
    lane = lax.broadcasted_iota(jnp.int32, rows.shape, 1)
    rows = jnp.where(lane < count_ref[0, g], rows, -1)
    node = lax.broadcasted_iota(jnp.int32, (nodes, rows.shape[1]), 0)
    return jnp.where(node == rows, 1.0, 0.0).astype(BF)


def pick_body(scalars, arrays, copies, outs):
    (count_ref,), (rows_ref, feat_ref), (out_ref,) = scalars, arrays, outs
    wait(copies)
    feat = feat_ref[...]
    for g in range(out_ref.shape[0]):
        hot = hot_columns(rows_ref, count_ref, g, feat.shape[0])
        out_ref[g] = lax.dot_general(hot, feat, TN, preferred_element_type=F32).astype(BF)


def spot_of(index_ref, t, k):
    index = index_ref[t, k]
    z, x = lax.shift_right_logical(index, 1) & (NZ - 1), lax.shift_right_logical(index, 4)
    return (z * NX + x) * 2 + (index & 1)


def main_body(
    scalars, arrays, copies, outs, gathered, tiles, acc, terms, tile_sem, term_sems
):
    index_ref, count_ref = scalars
    blocks_ref, outer_ref, pre_ref, w_ref, dout_ref, feat_ref, wself_ref, cut_ref = arrays
    out_ref, dagg_ref, back_ref, part_ref, self_ref, term_ref = outs
    tile_copy = pltpu.make_async_copy(gathered[0], tiles.at[pl.ds(0, 2 * BANDS)], tile_sem)
    tile_copy.start()
    slots = blocks_ref.shape[1]
    spare = 2 * BANDS
    tiles[spare] = jnp.zeros(tiles.shape[1:], BF)

    def clear(i, carry):
        acc[i] = jnp.zeros(acc.shape[1:], F32)
        return carry

    lax.fori_loop(0, spare, clear, 0)
    wait(copies)
    tile_copy.wait()
    aggs, d_pres, d_aggs = [], [], []
    for t in range(2):
        rows = pl.ds(t * 128, 128)
        spots = [
            jnp.where(k < count_ref[t], spot_of(index_ref, t, k), spare)
            for k in range(slots)
        ]
        total = outer_ref[rows, :]
        for k in range(0, slots, 2):
            left = jnp.concatenate([blocks_ref[t, k], blocks_ref[t, k + 1]], axis=1)
            right = jnp.concatenate([tiles[spots[k]], tiles[spots[k + 1]]], axis=0)
            total = total + jnp.dot(left, right, preferred_element_type=F32)
        agg = total.astype(BF)
        pre = pre_ref[rows, :] + jnp.dot(agg, w_ref[...], preferred_element_type=F32)
        sig = jax.nn.sigmoid(pre)
        out_ref[rows, :] = (pre * sig).astype(BF)
        d_pre = (dout_ref[rows, :].astype(F32) * sig * (1.0 + pre * (1.0 - sig))).astype(BF)
        d_agg = lax.dot_general(d_pre, w_ref[...], NT, preferred_element_type=F32).astype(BF)
        dagg_ref[rows, :] = d_agg
        for k in range(slots):
            term = lax.dot_general(blocks_ref[t, k], d_agg, TN, preferred_element_type=F32)
            acc[spots[k]] = acc[spots[k]] + term
        d_aggs.append(d_agg)
        aggs.append(agg)
        d_pres.append(d_pre)
    stores = []
    for c in range(STORE):
        part = pl.ds(c * (spare // STORE), spare // STORE)

        def convert(i, carry):
            terms[i] = acc[i].astype(BF)
            return carry

        lax.fori_loop(part.start, part.start + part.size, convert, 0)
        store = pltpu.make_async_copy(terms.at[part], term_ref.at[part], term_sems.at[c])
        store.start()
        stores.append(store)
    agg, d_pre = jnp.concatenate(aggs, axis=0), jnp.concatenate(d_pres, axis=0)
    width = d_pre.shape[1]
    groups = back_ref.shape[0]
    cut = cut_ref.shape[1] // groups
    share = part_ref.shape[1] - SPARE_ROWS
    grads = [
        lax.dot_general(left, d_pre, TN, preferred_element_type=F32).astype(BF)
        for left in (feat_ref[...], agg)
    ]
    bias = jnp.sum(d_pre.astype(F32), axis=0, keepdims=True)
    row = lax.broadcasted_iota(jnp.int32, (SPARE_ROWS, width), 0)
    bias = jnp.where(row == 0, bias, 0.0).astype(BF)
    for x in range(NX):
        grad, at = grads[2 * x // NX], x % 2 * share
        part_ref[x, pl.ds(0, share), :] = grad[at : at + share]
        part_ref[x, pl.ds(share, SPARE_ROWS), :] = bias
    d_agg = jnp.concatenate(d_aggs, axis=0)
    for g in range(0, groups, 2):
        rows = lax.dot_general(
            cut_ref[:, pl.ds(g * cut, 2 * cut)], d_agg, TN, preferred_element_type=F32
        ).astype(BF)
        back_ref[g, pl.ds(0, cut), :] = rows[:cut]
        back_ref[g + 1, pl.ds(0, cut), :] = rows[cut:]
    self_ref[...] = lax.dot_general(d_pre, wself_ref[...], NT, preferred_element_type=F32)
    wait(stores)


def blocks_body(scalars, arrays, copies, outs):
    (index_ref, count_ref), (dagg_ref, tiles), (out_ref,) = scalars, arrays, outs
    wait(copies)
    for t in range(2):
        d_agg = dagg_ref[pl.ds(t * 128, 128), :]
        for k in range(out_ref.shape[1]):
            live = jnp.where(k < count_ref[t], 1.0, 0.0)
            tile = tiles[spot_of(index_ref, t, k)]
            grad = lax.dot_general(d_agg, tile, NT, preferred_element_type=F32)
            out_ref[t, k] = (grad * live).astype(BF)


def base_body(scalars, arrays, copies, outs):
    (count_ref,), (rows_ref, back_ref, self_ref, *term_refs), (out_ref,) = scalars, arrays, outs
    wait(copies)
    total = self_ref[...]
    for term_ref in term_refs:
        total = total + term_ref[pl.ds(0, total.shape[0]), :].astype(F32)
    for g in range(0, back_ref.shape[0], 2):
        hot = jnp.concatenate(
            [hot_columns(rows_ref, count_ref, g + i, total.shape[0]) for i in range(2)], axis=1
        )
        rows = jnp.concatenate([back_ref[g], back_ref[g + 1]], axis=0)
        total = total + jnp.dot(hot, rows, preferred_element_type=F32)
    out_ref[...] = total.astype(BF)


def grads_body(scale, scalars, arrays, copies, outs):
    (x_ref,) = scalars
    wait(copies)
    share = sum(out_ref.shape[0] for out_ref in outs) // len(arrays)
    for by, rows_ref in enumerate(arrays):
        x = (x_ref[0] - by) & (NX - 1)
        grads = rows_ref[pl.ds(rows_ref.shape[0] - share, share), :].astype(F32) * scale
        for i, out_ref in enumerate(outs):
            held = out_ref.shape[0] // share

            @pl.when(lax.div(x, held) == i)
            def _(out_ref=out_ref, grads=grads, spot=(x & (held - 1)) * share):
                out_ref[pl.ds(pl.multiple_of(spot, share), share), :] = grads


def share_body(scalars, arrays, copies, outs):
    (parts_ref,), (out_ref,) = arrays, outs
    wait(copies)
    total = parts_ref[0].astype(F32)
    for i in range(1, parts_ref.shape[0]):
        total = total + parts_ref[i].astype(F32)
    total = total.astype(BF)
    share = out_ref.shape[1] - SPARE_ROWS
    last = total.shape[0] - SPARE_ROWS
    for i in range(out_ref.shape[0]):
        out_ref[i, pl.ds(0, share), :] = total[i * share : (i + 1) * share]
        out_ref[i, pl.ds(share, SPARE_ROWS), :] = total[last:]


def gate(x, after):
    return pl.pallas_call(
        lambda x_ref, after_ref, out_ref: None,
        out_shape=sds(x.shape, x.dtype),
        in_specs=[HBM, HBM],
        out_specs=HBM,
        input_output_aliases={0: 0},
        compiler_params=pltpu.CompilerParams(vmem_limit_bytes=60 << 20),
    )(x, after)


def a2a(x, axis):
    return lax.all_to_all(x, axis, 0, 0, tiled=True)


def shift(x, axis, n, by):
    return lax.ppermute(x, axis, [(i, (i + by) % n) for i in range(n)])


def local(
    features, block_index, block_count, block_values, cut_weight, send_rows, send_count,
    w_self, w_neigh, bias, d_out,
):
    nodes, width = features.shape
    tiles_here, slots = block_index.shape
    scale = 1.0 / math.sqrt(nodes * NG * BANDS)
    rows2 = send_rows.reshape(NG, -1)
    cut = rows2.shape[1]
    node_bf, node_f32 = sds((nodes, width), BF), sds((nodes, width), F32)
    cut_bf = sds((NG, cut, width), BF)

    gathered = lax.all_gather(features, "x", axis=0, tiled=True)
    gathered = lax.all_gather(gathered, "z", axis=0, tiled=True).reshape(2 * BANDS, 128, width)

    (outgoing,) = call(
        pick_body, [send_count], [rows2, features], [cut_bf], flops=2 * NG * cut * width * nodes,
    )
    arrived = a2a(outgoing, ("y", "c")).reshape(NG * cut, width)
    outer = jnp.dot(cut_weight, arrived, preferred_element_type=F32)
    own_pre = jnp.dot(features, w_self, preferred_element_type=F32) + bias

    outs = [
        node_bf, node_bf, cut_bf, sds((NX, 2 * width // NX + SPARE_ROWS, width), BF), node_f32,
        sds(gathered.shape, BF),
    ]
    spared = (2 * BANDS + 1, 128, width)
    output, d_agg, back, part, self_back, terms = call(
        main_body,
        [block_index, block_count],
        [block_values, outer, own_pre, w_neigh, d_out, features, w_self, cut_weight],
        outs,
        out_specs=[VMEM] * (len(outs) - 1) + [HBM],
        scratch=[
            pltpu.VMEM(spared, BF),
            pltpu.VMEM(spared, F32),
            pltpu.VMEM(gathered.shape, BF),
            pltpu.SemaphoreType.DMA,
            pltpu.SemaphoreType.DMA((STORE,)),
        ],
        direct=[gathered],
        flops=1 << 30,
    )

    terms = lax.psum_scatter(terms.reshape(NZ, NX * nodes, width), "z", scatter_dimension=0)
    terms = terms.reshape(NX, nodes, width)
    me = lax.axis_index("x")

    share = 2 * width // BANDS
    part = a2a(part, "x")
    (part,) = call(share_body, [], [part], [sds((NZ, share + SPARE_ROWS, width), BF)])
    part = jnp.sum(a2a(part, "z").astype(F32), axis=0).astype(BF)
    part = a2a(jnp.broadcast_to(part[None], (NG, *part.shape)), ("y", "c"))
    part = jnp.sum(part.astype(F32), axis=0).astype(BF)
    returned = a2a(gate(back, part), ("y", "c"))
    grads = lax.all_gather(part[:share], "z", axis=0, tiled=True)
    moved = []
    for by in range(NX):
        rows = lax.dynamic_index_in_dim(terms, (me + by) & (NX - 1), 0, keepdims=False)
        rows = jnp.concatenate([rows, grads], axis=0)
        moved.append(shift(rows, "x", NX, by) if by else rows)
    grad_self, grad_neigh = call(
        functools.partial(grads_body, scale), [me.astype(jnp.int32).reshape(1)], moved,
        [sds((width, width), F32)] * 2,
    )

    (grad_blocks,) = call(
        blocks_body, [block_index, block_count], [d_agg, gathered], [sds(block_values.shape, BF)],
        extra=[moved[0]], flops=2 * tiles_here * slots * 128 * 128 * width,
    )
    (d_features,) = call(
        base_body, [send_count], [rows2, returned, self_back, *moved], [node_bf],
        flops=2 * NG * cut * width * nodes,
    )

    return (
        output,
        d_features,
        grad_blocks,
        grad_self,
        grad_neigh,
        part[share].astype(F32) * scale,
    )


def solution(mesh):
    mesh = Mesh(mesh.devices.reshape(NY, NC, NX, NZ), ("y", "c", "x", "z"))
    rows = ("y", "c", "x", "z")
    split = [P(rows)] * 7 + [P()] * 3 + [P(rows)]
    return jax.shard_map(
        local,
        mesh=mesh,
        in_specs=tuple(split),
        out_specs=(P(rows), P(rows), P(rows), P(), P(), P()),
        check_vma=False,
    )
```

```python
import math

import jax
import jax.numpy as jnp
from jax import lax
from jax.experimental import pallas as pl
from jax.experimental.pallas import tpu as pltpu
from jax.sharding import Mesh, PartitionSpec as P

BF = jnp.bfloat16
F32 = jnp.float32
TN = (((0,), (0,)), ((), ()))
NT = (((1,), (1,)), ((), ()))
NX, NZ, NY, NC = 4, 8, 8, 2
NG = NY * NC
BANDS = NX * NZ
SPARE_ROWS = 16
STORE = 8
VMEM = pl.BlockSpec(memory_space=pltpu.VMEM)
SMEM = pl.BlockSpec(memory_space=pltpu.SMEM)
HBM = pl.BlockSpec(memory_space=pltpu.HBM)


def sds(shape, dtype):
    return jax.ShapeDtypeStruct(shape, dtype)


def call(
    body, scalars, arrays, outs, out_specs=None, scratch=(), direct=(), extra=(), flops=0, vmem=60
):
    count, first = len(arrays), len(scalars)

    def kernel(*refs):
        sources = refs[first : first + count]
        rest = refs[first + count :]
        given, rest = rest[: len(direct)], rest[len(direct) + len(extra) :]
        outputs, rest = rest[: len(outs)], rest[len(outs) :]
        buffers, sems, rest = rest[:count], rest[count], rest[count + 1 :]
        copies = [
            pltpu.make_async_copy(source, buffer, sems.at[i])
            for i, (source, buffer) in enumerate(zip(sources, buffers, strict=True))
        ]
        for copy in copies:
            copy.start()
        body(refs[:first], buffers, copies, outputs, *([given] if direct else []), *rest)

    nbytes = sum(a.size * a.dtype.itemsize for a in (*arrays, *outs, *direct))
    return pl.pallas_call(
        kernel,
        out_shape=tuple(outs),
        in_specs=[SMEM] * first + [HBM] * (count + len(direct) + len(extra)),
        out_specs=tuple(out_specs or [VMEM] * len(outs)),
        scratch_shapes=[
            *(pltpu.VMEM(a.shape, a.dtype) for a in arrays),
            pltpu.SemaphoreType.DMA((max(count, 1),)),
            *scratch,
        ],
        compiler_params=pltpu.CompilerParams(vmem_limit_bytes=vmem << 20),
        cost_estimate=pl.CostEstimate(flops=flops, bytes_accessed=nbytes, transcendentals=0),
    )(*scalars, *arrays, *direct, *extra)


def wait(copies):
    for copy in copies:
        copy.wait()


def hot_columns(rows_ref, count_ref, g, nodes):
    rows = rows_ref[g : g + 1, :]
    lane = lax.broadcasted_iota(jnp.int32, rows.shape, 1)
    rows = jnp.where(lane < count_ref[0, g], rows, -1)
    node = lax.broadcasted_iota(jnp.int32, (nodes, rows.shape[1]), 0)
    return jnp.where(node == rows, 1.0, 0.0).astype(BF)


def pick_body(scalars, arrays, copies, outs):
    (count_ref,), (rows_ref, feat_ref), (out_ref,) = scalars, arrays, outs
    wait(copies)
    feat = feat_ref[...]
    for g in range(out_ref.shape[0]):
        hot = hot_columns(rows_ref, count_ref, g, feat.shape[0])
        out_ref[g] = lax.dot_general(hot, feat, TN, preferred_element_type=F32).astype(BF)


def spot_of(index_ref, t, k):
    index = index_ref[t, k]
    z, x = lax.shift_right_logical(index, 1) & (NZ - 1), lax.shift_right_logical(index, 4)
    return (z * NX + x) * 2 + (index & 1)


def main_body(
    scalars, arrays, copies, outs, gathered, tiles, acc, terms, tile_sem, term_sems
):
    index_ref, count_ref = scalars
    blocks_ref, outer_ref, pre_ref, w_ref, dout_ref, feat_ref, wself_ref, cut_ref = arrays
    out_ref, dagg_ref, back_ref, self_ref, term_ref = outs
    tile_copy = pltpu.make_async_copy(gathered[0], tiles.at[pl.ds(0, 2 * BANDS)], tile_sem)
    tile_copy.start()
    slots = blocks_ref.shape[1]
    spare = 2 * BANDS
    tiles[spare] = jnp.zeros(tiles.shape[1:], BF)

    def clear(i, carry):
        acc[i] = jnp.zeros(acc.shape[1:], F32)
        return carry

    lax.fori_loop(0, spare, clear, 0)
    wait(copies)
    tile_copy.wait()
    aggs, d_pres, d_aggs = [], [], []
    for t in range(2):
        rows = pl.ds(t * 128, 128)
        spots = [
            jnp.where(k < count_ref[t], spot_of(index_ref, t, k), spare)
            for k in range(slots)
        ]
        total = outer_ref[rows, :]
        for k in range(0, slots, 2):
            left = jnp.concatenate([blocks_ref[t, k], blocks_ref[t, k + 1]], axis=1)
            right = jnp.concatenate([tiles[spots[k]], tiles[spots[k + 1]]], axis=0)
            total = total + jnp.dot(left, right, preferred_element_type=F32)
        agg = total.astype(BF)
        pre = pre_ref[rows, :] + jnp.dot(agg, w_ref[...], preferred_element_type=F32)
        sig = jax.nn.sigmoid(pre)
        out_ref[rows, :] = (pre * sig).astype(BF)
        d_pre = (dout_ref[rows, :].astype(F32) * sig * (1.0 + pre * (1.0 - sig))).astype(BF)
        d_agg = lax.dot_general(d_pre, w_ref[...], NT, preferred_element_type=F32).astype(BF)
        dagg_ref[rows, :] = d_agg
        for k in range(slots):
            term = lax.dot_general(blocks_ref[t, k], d_agg, TN, preferred_element_type=F32)
            acc[spots[k]] = acc[spots[k]] + term
        d_aggs.append(d_agg)
        aggs.append(agg)
        d_pres.append(d_pre)
    stores = []
    for c in range(STORE):
        part = pl.ds(c * (spare // STORE), spare // STORE)

        def convert(i, carry):
            terms[i] = acc[i].astype(BF)
            return carry

        lax.fori_loop(part.start, part.start + part.size, convert, 0)
        store = pltpu.make_async_copy(terms.at[part], term_ref.at[part], term_sems.at[c])
        store.start()
        stores.append(store)
    agg, d_pre = jnp.concatenate(aggs, axis=0), jnp.concatenate(d_pres, axis=0)
    width = d_pre.shape[1]
    groups = back_ref.shape[0]
    cut = cut_ref.shape[1] // groups
    share = 2 * width // groups
    for i, left in enumerate((feat_ref[...], agg)):
        grad = lax.dot_general(left, d_pre, TN, preferred_element_type=F32).astype(BF)
        for g in range(groups // 2):
            spot = i * groups // 2 + g
            back_ref[spot, pl.ds(cut, share), :] = grad[g * share : (g + 1) * share]
    bias = jnp.sum(d_pre.astype(F32), axis=0, keepdims=True)
    row = lax.broadcasted_iota(jnp.int32, (SPARE_ROWS, width), 0)
    bias = jnp.where(row == 0, bias, 0.0).astype(BF)
    for g in range(groups):
        back_ref[g, pl.ds(cut + share, SPARE_ROWS), :] = bias
    d_agg = jnp.concatenate(d_aggs, axis=0)
    for g in range(0, groups, 2):
        rows = lax.dot_general(
            cut_ref[:, pl.ds(g * cut, 2 * cut)], d_agg, TN, preferred_element_type=F32
        ).astype(BF)
        back_ref[g, pl.ds(0, cut), :] = rows[:cut]
        back_ref[g + 1, pl.ds(0, cut), :] = rows[cut:]
    self_ref[...] = lax.dot_general(d_pre, wself_ref[...], NT, preferred_element_type=F32)
    wait(stores)


def blocks_body(scalars, arrays, copies, outs):
    (index_ref, count_ref), (dagg_ref, tiles), (out_ref,) = scalars, arrays, outs
    wait(copies)
    for t in range(2):
        d_agg = dagg_ref[pl.ds(t * 128, 128), :]
        for k in range(out_ref.shape[1]):
            live = jnp.where(k < count_ref[t], 1.0, 0.0)
            tile = tiles[spot_of(index_ref, t, k)]
            grad = lax.dot_general(d_agg, tile, NT, preferred_element_type=F32)
            out_ref[t, k] = (grad * live).astype(BF)


def base_body(scalars, arrays, copies, outs):
    (count_ref,), (rows_ref, back_ref, self_ref), (out_ref,) = scalars, arrays, outs
    cut = rows_ref.shape[1]
    wait(copies)
    total = self_ref[...]
    for g in range(0, back_ref.shape[0], 2):
        hot = jnp.concatenate(
            [hot_columns(rows_ref, count_ref, g + i, total.shape[0]) for i in range(2)], axis=1
        )
        rows = jnp.concatenate([back_ref[g + i, pl.ds(0, cut), :] for i in range(2)], axis=0)
        total = total + jnp.dot(hot, rows, preferred_element_type=F32)
    out_ref[...] = total


def behind_body(scalars, arrays, copies, outs, returned, parts_ref, sem):
    rows = parts_ref.shape[1]
    first = returned[0].shape[1] - rows
    copy = pltpu.make_async_copy(returned[0].at[:, pl.ds(first, rows)], parts_ref, sem)
    copy.start()
    sum_body(scalars, (parts_ref,), [copy], outs)


def sum_body(scalars, arrays, copies, outs):
    (parts_ref,), (out_ref,) = arrays, outs
    wait(copies)
    total = parts_ref[0].astype(F32)
    for i in range(1, parts_ref.shape[0]):
        total = total + parts_ref[i].astype(F32)
    for i in range(out_ref.shape[0]):
        out_ref[i] = total.astype(BF)


def a2a(x, axis):
    return lax.all_to_all(x, axis, 0, 0, tiled=True)


def shift(x, axis, n, by):
    return lax.ppermute(x, axis, [(i, (i + by) % n) for i in range(n)])


def local(
    features, block_index, block_count, block_values, cut_weight, send_rows, send_count,
    w_self, w_neigh, bias, d_out,
):
    nodes, width = features.shape
    tiles_here, slots = block_index.shape
    scale = 1.0 / math.sqrt(nodes * NG * BANDS)
    rows2 = send_rows.reshape(NG, -1)
    cut = rows2.shape[1]
    node_bf, node_f32 = sds((nodes, width), BF), sds((nodes, width), F32)
    cut_bf = sds((NG, cut, width), BF)

    gathered = lax.all_gather(features, "x", axis=0, tiled=True)
    gathered = lax.all_gather(gathered, "z", axis=0, tiled=True).reshape(2 * BANDS, 128, width)

    (outgoing,) = call(
        pick_body, [send_count], [rows2, features], [cut_bf], flops=2 * NG * cut * width * nodes,
    )
    arrived = a2a(outgoing, ("y", "c")).reshape(NG * cut, width)
    outer = jnp.dot(cut_weight, arrived, preferred_element_type=F32)
    own_pre = jnp.dot(features, w_self, preferred_element_type=F32) + bias

    share = 2 * width // NG
    outs = [
        node_bf, node_bf, sds((NG, cut + share + SPARE_ROWS, width), BF), node_f32,
        sds(gathered.shape, BF),
    ]
    spared = (2 * BANDS + 1, 128, width)
    output, d_agg, back, self_back, terms = call(
        main_body,
        [block_index, block_count],
        [block_values, outer, own_pre, w_neigh, d_out, features, w_self, cut_weight],
        outs,
        out_specs=[VMEM] * (len(outs) - 1) + [HBM],
        scratch=[
            pltpu.VMEM(spared, BF),
            pltpu.VMEM(spared, F32),
            pltpu.VMEM(gathered.shape, BF),
            pltpu.SemaphoreType.DMA,
            pltpu.SemaphoreType.DMA((STORE,)),
        ],
        direct=[gathered],
        flops=1 << 30,
    )

    terms = lax.psum_scatter(terms.reshape(NZ, NX * nodes, width), "z", scatter_dimension=0)
    terms = terms.reshape(NX, nodes, width)
    me = lax.axis_index("x")

    returned = a2a(back, ("y", "c"))
    (grad_blocks,) = call(
        blocks_body, [block_index, block_count], [d_agg, gathered], [sds(block_values.shape, BF)],
        flops=2 * tiles_here * slots * 128 * 128 * width,
    )
    (part,) = call(
        behind_body, [], [], [sds((NX, share + SPARE_ROWS, width), BF)],
        scratch=[pltpu.VMEM((NG, share + SPARE_ROWS, width), BF), pltpu.SemaphoreType.DMA],
        direct=[returned], extra=[grad_blocks],
    )
    part = a2a(part, "x")
    part = jnp.sum(part.astype(F32), axis=0).astype(BF)
    part = a2a(jnp.broadcast_to(part[None], (NZ, *part.shape)), "z")
    moved = []
    for by in range(NX):
        rows = lax.dynamic_index_in_dim(terms, (me + by) & (NX - 1), 0, keepdims=False)
        moved.append(shift(rows, "x", NX, by) if by else rows)
    (base,) = call(
        base_body, [send_count], [rows2, returned, self_back], [node_f32],
        flops=2 * NG * cut * width * nodes,
    )
    (part,) = call(
        sum_body, [], [part], [sds((NY, share + SPARE_ROWS, width), BF)], extra=[base, terms]
    )
    part = a2a(part, "y")
    grads = lax.all_gather(part, "c", axis=1).reshape(NG, share + SPARE_ROWS, width)
    grads = grads.astype(F32) * scale
    weight_grads = grads[:, :share].reshape(2, width, width)

    d_features = (base + sum(rows.astype(F32) for rows in moved)).astype(BF)

    return (
        output,
        d_features,
        grad_blocks,
        weight_grads[0],
        weight_grads[1],
        grads[0, share],
    )


def solution(mesh):
    mesh = Mesh(mesh.devices.reshape(NY, NC, NX, NZ), ("y", "c", "x", "z"))
    rows = ("y", "c", "x", "z")
    split = [P(rows)] * 7 + [P()] * 3 + [P(rows)]
    return jax.shard_map(
        local,
        mesh=mesh,
        in_specs=tuple(split),
        out_specs=(P(rows), P(rows), P(rows), P(), P(), P()),
        check_vma=False,
    )
```

```python
import math

import jax
import jax.numpy as jnp
from jax import lax
from jax.experimental import pallas as pl
from jax.experimental.pallas import tpu as pltpu
from jax.sharding import Mesh, PartitionSpec as P

BF = jnp.bfloat16
F32 = jnp.float32
TN = (((0,), (0,)), ((), ()))
NT = (((1,), (1,)), ((), ()))
NX, NZ, NY, NC = 4, 8, 8, 2
NG = NY * NC
BANDS = NX * NZ
SPARE_ROWS = 16
STORE = 8
VMEM = pl.BlockSpec(memory_space=pltpu.VMEM)
SMEM = pl.BlockSpec(memory_space=pltpu.SMEM)
HBM = pl.BlockSpec(memory_space=pltpu.HBM)


def sds(shape, dtype):
    return jax.ShapeDtypeStruct(shape, dtype)


def call(
    body, scalars, arrays, outs, out_specs=None, scratch=(), direct=(), extra=(), flops=0, vmem=63
):
    count, first = len(arrays), len(scalars)

    def kernel(*refs):
        sources = refs[first : first + count]
        rest = refs[first + count :]
        given, rest = rest[: len(direct)], rest[len(direct) + len(extra) :]
        outputs, rest = rest[: len(outs)], rest[len(outs) :]
        buffers, sems, rest = rest[:count], rest[count], rest[count + 1 :]
        copies = [
            pltpu.make_async_copy(source, buffer, sems.at[i])
            for i, (source, buffer) in enumerate(zip(sources, buffers, strict=True))
        ]
        for copy in copies:
            copy.start()
        body(refs[:first], buffers, copies, outputs, *([given] if direct else []), *rest)

    nbytes = sum(a.size * a.dtype.itemsize for a in (*arrays, *outs, *direct))
    return pl.pallas_call(
        kernel,
        out_shape=tuple(outs),
        in_specs=[SMEM] * first + [HBM] * (count + len(direct) + len(extra)),
        out_specs=tuple(out_specs or [VMEM] * len(outs)),
        scratch_shapes=[
            *(pltpu.VMEM(a.shape, a.dtype) for a in arrays),
            pltpu.SemaphoreType.DMA((max(count, 1),)),
            *scratch,
        ],
        compiler_params=pltpu.CompilerParams(vmem_limit_bytes=vmem << 20),
        cost_estimate=pl.CostEstimate(flops=flops, bytes_accessed=nbytes, transcendentals=0),
    )(*scalars, *arrays, *direct, *extra)


def wait(copies):
    for copy in copies:
        copy.wait()


def hot_columns(rows_ref, count_ref, g, nodes):
    rows = rows_ref[g : g + 1, :]
    lane = lax.broadcasted_iota(jnp.int32, rows.shape, 1)
    rows = jnp.where(lane < count_ref[0, g], rows, -1)
    node = lax.broadcasted_iota(jnp.int32, (nodes, rows.shape[1]), 0)
    return jnp.where(node == rows, 1.0, 0.0).astype(BF)


def pick_body(scalars, arrays, copies, outs):
    (count_ref,), (rows_ref, feat_ref), (out_ref,) = scalars, arrays, outs
    wait(copies)
    feat = feat_ref[...]
    for g in range(out_ref.shape[0]):
        hot = hot_columns(rows_ref, count_ref, g, feat.shape[0])
        out_ref[g] = lax.dot_general(hot, feat, TN, preferred_element_type=F32).astype(BF)


def spot_of(index_ref, t, k):
    index = index_ref[t, k]
    z, x = lax.shift_right_logical(index, 1) & (NZ - 1), lax.shift_right_logical(index, 4)
    return (z * NX + x) * 2 + (index & 1)


def main_body(
    scalars, arrays, copies, outs, gathered, tiles, acc, terms, tile_sem, term_sems
):
    index_ref, count_ref = scalars
    blocks_ref, outer_ref, pre_ref, w_ref, dout_ref, feat_ref, wself_ref, cut_ref = arrays
    out_ref, dagg_ref, back_ref, self_ref, term_ref = outs
    tile_copy = pltpu.make_async_copy(gathered[0], tiles.at[pl.ds(0, 2 * BANDS)], tile_sem)
    tile_copy.start()
    slots = blocks_ref.shape[1]
    spare = 2 * BANDS
    tiles[spare] = jnp.zeros(tiles.shape[1:], BF)

    def clear(i, carry):
        acc[i] = jnp.zeros(acc.shape[1:], F32)
        return carry

    lax.fori_loop(0, spare, clear, 0)
    wait(copies)
    tile_copy.wait()
    aggs, d_pres, d_aggs = [], [], []
    for t in range(2):
        rows = pl.ds(t * 128, 128)
        spots = [
            jnp.where(k < count_ref[t], spot_of(index_ref, t, k), spare)
            for k in range(slots)
        ]
        total = outer_ref[rows, :]
        for k in range(0, slots, 2):
            left = jnp.concatenate([blocks_ref[t, k], blocks_ref[t, k + 1]], axis=1)
            right = jnp.concatenate([tiles[spots[k]], tiles[spots[k + 1]]], axis=0)
            total = total + jnp.dot(left, right, preferred_element_type=F32)
        agg = total.astype(BF)
        pre = pre_ref[rows, :] + jnp.dot(agg, w_ref[...], preferred_element_type=F32)
        sig = jax.nn.sigmoid(pre)
        out_ref[rows, :] = (pre * sig).astype(BF)
        d_pre = (dout_ref[rows, :].astype(F32) * sig * (1.0 + pre * (1.0 - sig))).astype(BF)
        d_agg = lax.dot_general(d_pre, w_ref[...], NT, preferred_element_type=F32).astype(BF)
        dagg_ref[rows, :] = d_agg
        for k in range(slots):
            term = lax.dot_general(blocks_ref[t, k], d_agg, TN, preferred_element_type=F32)
            acc[spots[k]] = acc[spots[k]] + term
        d_aggs.append(d_agg)
        aggs.append(agg)
        d_pres.append(d_pre)
    stores = []
    for c in range(STORE):
        part = pl.ds(c * (spare // STORE), spare // STORE)

        def convert(i, carry):
            terms[i] = acc[i].astype(BF)
            return carry

        lax.fori_loop(part.start, part.start + part.size, convert, 0)
        store = pltpu.make_async_copy(terms.at[part], term_ref.at[part], term_sems.at[c])
        store.start()
        stores.append(store)
    agg, d_pre = jnp.concatenate(aggs, axis=0), jnp.concatenate(d_pres, axis=0)
    width = d_pre.shape[1]
    groups = back_ref.shape[0]
    cut = cut_ref.shape[1] // groups
    share = 2 * width // groups
    for i, left in enumerate((feat_ref[...], agg)):
        grad = lax.dot_general(left, d_pre, TN, preferred_element_type=F32).astype(BF)
        for g in range(groups // 2):
            spot = i * groups // 2 + g
            back_ref[spot, pl.ds(cut, share), :] = grad[g * share : (g + 1) * share]
    bias = jnp.sum(d_pre.astype(F32), axis=0, keepdims=True)
    row = lax.broadcasted_iota(jnp.int32, (SPARE_ROWS, width), 0)
    bias = jnp.where(row == 0, bias, 0.0).astype(BF)
    for g in range(groups):
        back_ref[g, pl.ds(cut + share, SPARE_ROWS), :] = bias
    d_agg = jnp.concatenate(d_aggs, axis=0)
    for g in range(0, groups, 2):
        rows = lax.dot_general(
            cut_ref[:, pl.ds(g * cut, 2 * cut)], d_agg, TN, preferred_element_type=F32
        ).astype(BF)
        back_ref[g, pl.ds(0, cut), :] = rows[:cut]
        back_ref[g + 1, pl.ds(0, cut), :] = rows[cut:]
    self_ref[...] = lax.dot_general(d_pre, wself_ref[...], NT, preferred_element_type=F32)
    wait(stores)


def blocks_body(scalars, arrays, copies, outs):
    (index_ref, count_ref), (dagg_ref, tiles), (out_ref,) = scalars, arrays, outs
    wait(copies)
    for t in range(2):
        d_agg = dagg_ref[pl.ds(t * 128, 128), :]
        for k in range(out_ref.shape[1]):
            live = jnp.where(k < count_ref[t], 1.0, 0.0)
            tile = tiles[spot_of(index_ref, t, k)]
            grad = lax.dot_general(d_agg, tile, NT, preferred_element_type=F32)
            out_ref[t, k] = (grad * live).astype(BF)


def base_body(scalars, arrays, copies, outs):
    (count_ref,), (rows_ref, back_ref, self_ref), (out_ref,) = scalars, arrays, outs
    cut = rows_ref.shape[1]
    wait(copies)
    total = self_ref[...]
    for g in range(0, back_ref.shape[0], 2):
        hot = jnp.concatenate(
            [hot_columns(rows_ref, count_ref, g + i, total.shape[0]) for i in range(2)], axis=1
        )
        rows = jnp.concatenate([back_ref[g + i, pl.ds(0, cut), :] for i in range(2)], axis=0)
        total = total + jnp.dot(hot, rows, preferred_element_type=F32)
    out_ref[...] = total


def behind_body(scalars, arrays, copies, outs, returned, parts_ref, sem):
    rows = parts_ref.shape[1]
    first = returned[0].shape[1] - rows
    copy = pltpu.make_async_copy(returned[0].at[:, pl.ds(first, rows)], parts_ref, sem)
    copy.start()
    sum_body(scalars, (parts_ref,), [copy], outs)


def sum_body(scalars, arrays, copies, outs):
    (parts_ref,), (out_ref,) = arrays, outs
    wait(copies)
    total = parts_ref[0].astype(F32)
    for i in range(1, parts_ref.shape[0]):
        total = total + parts_ref[i].astype(F32)
    for i in range(out_ref.shape[0]):
        out_ref[i] = total.astype(BF)


def a2a(x, axis):
    return lax.all_to_all(x, axis, 0, 0, tiled=True)


def shift(x, axis, n, by):
    return lax.ppermute(x, axis, [(i, (i + by) % n) for i in range(n)])


def local(
    features, block_index, block_count, block_values, cut_weight, send_rows, send_count,
    w_self, w_neigh, bias, d_out,
):
    nodes, width = features.shape
    tiles_here, slots = block_index.shape
    scale = 1.0 / math.sqrt(nodes * NG * BANDS)
    rows2 = send_rows.reshape(NG, -1)
    cut = rows2.shape[1]
    node_bf, node_f32 = sds((nodes, width), BF), sds((nodes, width), F32)
    cut_bf = sds((NG, cut, width), BF)

    gathered = lax.all_gather(features, "x", axis=0, tiled=True)
    gathered = lax.all_gather(gathered, "z", axis=0, tiled=True).reshape(2 * BANDS, 128, width)

    (outgoing,) = call(
        pick_body, [send_count], [rows2, features], [cut_bf], flops=2 * NG * cut * width * nodes,
    )
    arrived = a2a(outgoing, ("y", "c")).reshape(NG * cut, width)
    outer = jnp.dot(cut_weight, arrived, preferred_element_type=F32)
    own_pre = jnp.dot(features, w_self, preferred_element_type=F32) + bias

    share = 2 * width // NG
    outs = [
        node_bf, node_bf, sds((NG, cut + share + SPARE_ROWS, width), BF), node_f32,
        sds(gathered.shape, BF),
    ]
    spared = (2 * BANDS + 1, 128, width)
    output, d_agg, back, self_back, terms = call(
        main_body,
        [block_index, block_count],
        [block_values, outer, own_pre, w_neigh, d_out, features, w_self, cut_weight],
        outs,
        out_specs=[VMEM] * (len(outs) - 1) + [HBM],
        scratch=[
            pltpu.VMEM(spared, BF),
            pltpu.VMEM(spared, F32),
            pltpu.VMEM(gathered.shape, BF),
            pltpu.SemaphoreType.DMA,
            pltpu.SemaphoreType.DMA((STORE,)),
        ],
        direct=[gathered],
        flops=1 << 30,
    )

    terms = lax.psum_scatter(terms.reshape(NZ, NX * nodes, width), "z", scatter_dimension=0)
    terms = terms.reshape(NX, nodes, width)
    me = lax.axis_index("x")

    returned = a2a(back, ("y", "c"))
    (grad_blocks,) = call(
        blocks_body, [block_index, block_count], [d_agg, gathered], [sds(block_values.shape, BF)],
        flops=2 * tiles_here * slots * 128 * 128 * width,
    )
    (part,) = call(
        behind_body, [], [], [sds((NX, share + SPARE_ROWS, width), BF)],
        scratch=[pltpu.VMEM((NG, share + SPARE_ROWS, width), BF), pltpu.SemaphoreType.DMA],
        direct=[returned], extra=[grad_blocks],
    )
    part = a2a(part, "x")
    part = jnp.sum(part.astype(F32), axis=0).astype(BF)
    part = a2a(jnp.broadcast_to(part[None], (NZ, *part.shape)), "z")
    moved = []
    for by in range(NX):
        rows = lax.dynamic_index_in_dim(terms, (me + by) & (NX - 1), 0, keepdims=False)
        moved.append(shift(rows, "x", NX, by) if by else rows)
    (base,) = call(
        base_body, [send_count], [rows2, returned, self_back], [node_f32],
        flops=2 * NG * cut * width * nodes,
    )
    (part,) = call(
        sum_body, [], [part], [sds((NY, share + SPARE_ROWS, width), BF)], extra=[terms]
    )
    part = a2a(part, "y")
    grads = lax.all_gather(part, "c", axis=1).reshape(NG, share + SPARE_ROWS, width)
    grads = grads.astype(F32) * scale
    weight_grads = grads[:, :share].reshape(2, width, width)

    d_features = (base + sum(rows.astype(F32) for rows in moved)).astype(BF)

    return (
        output,
        d_features,
        grad_blocks,
        weight_grads[0],
        weight_grads[1],
        grads[0, share],
    )


def solution(mesh):
    mesh = Mesh(mesh.devices.reshape(NY, NC, NX, NZ), ("y", "c", "x", "z"))
    rows = ("y", "c", "x", "z")
    split = [P(rows)] * 7 + [P()] * 3 + [P(rows)]
    return jax.shard_map(
        local,
        mesh=mesh,
        in_specs=tuple(split),
        out_specs=(P(rows), P(rows), P(rows), P(), P(), P()),
        check_vma=False,
    )
```

```python
import math

import jax
import jax.numpy as jnp
from jax import lax
from jax.experimental import pallas as pl
from jax.experimental.pallas import tpu as pltpu
from jax.sharding import Mesh, PartitionSpec as P

BF = jnp.bfloat16
F32 = jnp.float32
TN = (((0,), (0,)), ((), ()))
NT = (((1,), (1,)), ((), ()))
NX, NZ, NY, NC = 4, 8, 8, 2
NG = NY * NC
BANDS = NX * NZ
SPARE_ROWS = 16
STORE = 8
VMEM = pl.BlockSpec(memory_space=pltpu.VMEM)
SMEM = pl.BlockSpec(memory_space=pltpu.SMEM)
HBM = pl.BlockSpec(memory_space=pltpu.HBM)


def sds(shape, dtype):
    return jax.ShapeDtypeStruct(shape, dtype)


def call(
    body, scalars, arrays, outs, out_specs=None, scratch=(), direct=(), extra=(), flops=0, vmem=63
):
    count, first = len(arrays), len(scalars)

    def kernel(*refs):
        sources = refs[first : first + count]
        rest = refs[first + count :]
        given, rest = rest[: len(direct)], rest[len(direct) + len(extra) :]
        outputs, rest = rest[: len(outs)], rest[len(outs) :]
        buffers, sems, rest = rest[:count], rest[count], rest[count + 1 :]
        copies = [
            pltpu.make_async_copy(source, buffer, sems.at[i])
            for i, (source, buffer) in enumerate(zip(sources, buffers, strict=True))
        ]
        for copy in copies:
            copy.start()
        body(refs[:first], buffers, copies, outputs, *([given] if direct else []), *rest)

    nbytes = sum(a.size * a.dtype.itemsize for a in (*arrays, *outs, *direct))
    return pl.pallas_call(
        kernel,
        out_shape=tuple(outs),
        in_specs=[SMEM] * first + [HBM] * (count + len(direct) + len(extra)),
        out_specs=tuple(out_specs or [VMEM] * len(outs)),
        scratch_shapes=[
            *(pltpu.VMEM(a.shape, a.dtype) for a in arrays),
            pltpu.SemaphoreType.DMA((max(count, 1),)),
            *scratch,
        ],
        compiler_params=pltpu.CompilerParams(vmem_limit_bytes=vmem << 20),
        cost_estimate=pl.CostEstimate(flops=flops, bytes_accessed=nbytes, transcendentals=0),
    )(*scalars, *arrays, *direct, *extra)


def wait(copies):
    for copy in copies:
        copy.wait()


def hot_columns(rows_ref, count_ref, g, nodes):
    rows = rows_ref[g : g + 1, :]
    lane = lax.broadcasted_iota(jnp.int32, rows.shape, 1)
    rows = jnp.where(lane < count_ref[0, g], rows, -1)
    node = lax.broadcasted_iota(jnp.int32, (nodes, rows.shape[1]), 0)
    return jnp.where(node == rows, 1.0, 0.0).astype(BF)


def pick_body(scalars, arrays, copies, outs):
    (count_ref,), (rows_ref, feat_ref), (out_ref,) = scalars, arrays, outs
    wait(copies)
    feat = feat_ref[...]
    for g in range(out_ref.shape[0]):
        hot = hot_columns(rows_ref, count_ref, g, feat.shape[0])
        out_ref[g] = lax.dot_general(hot, feat, TN, preferred_element_type=F32).astype(BF)


def spot_of(index_ref, t, k):
    index = index_ref[t, k]
    z, x = lax.shift_right_logical(index, 1) & (NZ - 1), lax.shift_right_logical(index, 4)
    return (z * NX + x) * 2 + (index & 1)


def main_body(
    scalars, arrays, copies, outs, gathered, tiles, acc, terms, tile_sem, term_sems
):
    index_ref, count_ref = scalars
    blocks_ref, outer_ref, pre_ref, w_ref, dout_ref, feat_ref, wself_ref, cut_ref = arrays
    out_ref, dagg_ref, back_ref, part_ref, self_ref, term_ref = outs
    tile_copy = pltpu.make_async_copy(gathered[0], tiles.at[pl.ds(0, 2 * BANDS)], tile_sem)
    tile_copy.start()
    slots = blocks_ref.shape[1]
    spare = 2 * BANDS
    tiles[spare] = jnp.zeros(tiles.shape[1:], BF)

    def clear(i, carry):
        acc[i] = jnp.zeros(acc.shape[1:], F32)
        return carry

    lax.fori_loop(0, spare, clear, 0)
    wait(copies)
    tile_copy.wait()
    aggs, d_pres, d_aggs = [], [], []
    for t in range(2):
        rows = pl.ds(t * 128, 128)
        spots = [
            jnp.where(k < count_ref[t], spot_of(index_ref, t, k), spare)
            for k in range(slots)
        ]
        total = outer_ref[rows, :]
        for k in range(0, slots, 2):
            left = jnp.concatenate([blocks_ref[t, k], blocks_ref[t, k + 1]], axis=1)
            right = jnp.concatenate([tiles[spots[k]], tiles[spots[k + 1]]], axis=0)
            total = total + jnp.dot(left, right, preferred_element_type=F32)
        agg = total.astype(BF)
        pre = pre_ref[rows, :] + jnp.dot(agg, w_ref[...], preferred_element_type=F32)
        sig = jax.nn.sigmoid(pre)
        out_ref[rows, :] = (pre * sig).astype(BF)
        d_pre = (dout_ref[rows, :].astype(F32) * sig * (1.0 + pre * (1.0 - sig))).astype(BF)
        d_agg = lax.dot_general(d_pre, w_ref[...], NT, preferred_element_type=F32).astype(BF)
        dagg_ref[rows, :] = d_agg
        for k in range(slots):
            term = lax.dot_general(blocks_ref[t, k], d_agg, TN, preferred_element_type=F32)
            acc[spots[k]] = acc[spots[k]] + term
        d_aggs.append(d_agg)
        aggs.append(agg)
        d_pres.append(d_pre)
    stores = []
    for c in range(STORE):
        part = pl.ds(c * (spare // STORE), spare // STORE)

        def convert(i, carry):
            terms[i] = acc[i].astype(BF)
            return carry

        lax.fori_loop(part.start, part.start + part.size, convert, 0)
        store = pltpu.make_async_copy(terms.at[part], term_ref.at[part], term_sems.at[c])
        store.start()
        stores.append(store)
    agg, d_pre = jnp.concatenate(aggs, axis=0), jnp.concatenate(d_pres, axis=0)
    width = d_pre.shape[1]
    groups = back_ref.shape[0]
    cut = cut_ref.shape[1] // groups
    share = 2 * width // groups
    for i, left in enumerate((feat_ref[...], agg)):
        grad = lax.dot_general(left, d_pre, TN, preferred_element_type=F32).astype(BF)
        for g in range(groups // 2):
            spot = i * groups // 2 + g
            part_ref[spot, pl.ds(0, share), :] = grad[g * share : (g + 1) * share]
    bias = jnp.sum(d_pre.astype(F32), axis=0, keepdims=True)
    row = lax.broadcasted_iota(jnp.int32, (SPARE_ROWS, width), 0)
    bias = jnp.where(row == 0, bias, 0.0).astype(BF)
    for g in range(groups):
        part_ref[g, pl.ds(share, SPARE_ROWS), :] = bias
    d_agg = jnp.concatenate(d_aggs, axis=0)
    for g in range(0, groups, 2):
        rows = lax.dot_general(
            cut_ref[:, pl.ds(g * cut, 2 * cut)], d_agg, TN, preferred_element_type=F32
        ).astype(BF)
        back_ref[g] = rows[:cut]
        back_ref[g + 1] = rows[cut:]
    self_ref[...] = lax.dot_general(d_pre, wself_ref[...], NT, preferred_element_type=F32)
    wait(stores)


def blocks_body(scalars, arrays, copies, outs):
    (index_ref, count_ref), (dagg_ref, tiles), (out_ref,) = scalars, arrays, outs
    wait(copies)
    for t in range(2):
        d_agg = dagg_ref[pl.ds(t * 128, 128), :]
        for k in range(out_ref.shape[1]):
            live = jnp.where(k < count_ref[t], 1.0, 0.0)
            tile = tiles[spot_of(index_ref, t, k)]
            grad = lax.dot_general(d_agg, tile, NT, preferred_element_type=F32)
            out_ref[t, k] = (grad * live).astype(BF)


def base_body(scalars, arrays, copies, outs):
    (count_ref,), (rows_ref, back_ref, self_ref), (out_ref,) = scalars, arrays, outs
    wait(copies)
    total = self_ref[...]
    for g in range(0, back_ref.shape[0], 2):
        hot = jnp.concatenate(
            [hot_columns(rows_ref, count_ref, g + i, total.shape[0]) for i in range(2)], axis=1
        )
        rows = jnp.concatenate([back_ref[g], back_ref[g + 1]], axis=0)
        total = total + jnp.dot(hot, rows, preferred_element_type=F32)
    out_ref[...] = total


def sum_body(scalars, arrays, copies, outs):
    (parts_ref,), (out_ref,) = arrays, outs
    wait(copies)
    total = parts_ref[0].astype(F32)
    for i in range(1, parts_ref.shape[0]):
        total = total + parts_ref[i].astype(F32)
    for i in range(out_ref.shape[0]):
        out_ref[i] = total.astype(BF)


def gate(x, after):
    return pl.pallas_call(
        lambda x_ref, after_ref, out_ref: None,
        out_shape=sds(x.shape, x.dtype),
        in_specs=[HBM, HBM],
        out_specs=HBM,
        input_output_aliases={0: 0},
        compiler_params=pltpu.CompilerParams(vmem_limit_bytes=63 << 20),
    )(x, after)


def a2a(x, axis):
    return lax.all_to_all(x, axis, 0, 0, tiled=True)


def shift(x, axis, n, by):
    return lax.ppermute(x, axis, [(i, (i + by) % n) for i in range(n)])


def local(
    features, block_index, block_count, block_values, cut_weight, send_rows, send_count,
    w_self, w_neigh, bias, d_out,
):
    nodes, width = features.shape
    tiles_here, slots = block_index.shape
    scale = 1.0 / math.sqrt(nodes * NG * BANDS)
    rows2 = send_rows.reshape(NG, -1)
    cut = rows2.shape[1]
    node_bf, node_f32 = sds((nodes, width), BF), sds((nodes, width), F32)
    cut_bf = sds((NG, cut, width), BF)

    gathered = lax.all_gather(features, "x", axis=0, tiled=True)
    gathered = lax.all_gather(gathered, "z", axis=0, tiled=True).reshape(2 * BANDS, 128, width)

    (outgoing,) = call(
        pick_body, [send_count], [rows2, features], [cut_bf], flops=2 * NG * cut * width * nodes,
    )
    arrived = a2a(outgoing, ("y", "c")).reshape(NG * cut, width)
    outer = jnp.dot(cut_weight, arrived, preferred_element_type=F32)
    own_pre = jnp.dot(features, w_self, preferred_element_type=F32) + bias

    share = 2 * width // NG
    outs = [
        node_bf, node_bf, cut_bf, sds((NG, share + SPARE_ROWS, width), BF), node_f32,
        sds(gathered.shape, BF),
    ]
    spared = (2 * BANDS + 1, 128, width)
    output, d_agg, back, part, self_back, terms = call(
        main_body,
        [block_index, block_count],
        [block_values, outer, own_pre, w_neigh, d_out, features, w_self, cut_weight],
        outs,
        out_specs=[VMEM] * (len(outs) - 1) + [HBM],
        scratch=[
            pltpu.VMEM(spared, BF),
            pltpu.VMEM(spared, F32),
            pltpu.VMEM(gathered.shape, BF),
            pltpu.SemaphoreType.DMA,
            pltpu.SemaphoreType.DMA((STORE,)),
        ],
        direct=[gathered],
        flops=1 << 30,
    )

    terms = lax.psum_scatter(terms.reshape(NZ, NX * nodes, width), "z", scatter_dimension=0)
    terms = terms.reshape(NX, nodes, width)
    me = lax.axis_index("x")

    part = jnp.sum(a2a(part, ("y", "c")).astype(F32), axis=0).astype(BF)
    returned = a2a(gate(back, part), ("y", "c"))
    part = lax.all_gather(part, "x", axis=0)
    (grad_blocks,) = call(
        blocks_body, [block_index, block_count], [d_agg, gathered], [sds(block_values.shape, BF)],
        flops=2 * tiles_here * slots * 128 * 128 * width,
    )
    (part,) = call(
        sum_body, [], [part], [sds((NZ, share + SPARE_ROWS, width), BF)],
        extra=[returned, grad_blocks],
    )
    part = a2a(part, "z")
    moved = []
    for by in range(NX):
        rows = lax.dynamic_index_in_dim(terms, (me + by) & (NX - 1), 0, keepdims=False)
        moved.append(shift(rows, "x", NX, by) if by else rows)
    (base,) = call(
        base_body, [send_count], [rows2, returned, self_back], [node_f32],
        flops=2 * NG * cut * width * nodes,
    )
    (part,) = call(
        sum_body, [], [part], [sds((NY, share + SPARE_ROWS, width), BF)], extra=[terms]
    )
    part = a2a(part, "y")
    grads = lax.all_gather(part, "c", axis=1).reshape(NG, share + SPARE_ROWS, width)
    grads = grads.astype(F32) * scale
    weight_grads = grads[:, :share].reshape(2, width, width)

    d_features = (base + sum(rows.astype(F32) for rows in moved)).astype(BF)

    return (
        output,
        d_features,
        grad_blocks,
        weight_grads[0],
        weight_grads[1],
        grads[0, share],
    )


def solution(mesh):
    mesh = Mesh(mesh.devices.reshape(NY, NC, NX, NZ), ("y", "c", "x", "z"))
    rows = ("y", "c", "x", "z")
    split = [P(rows)] * 7 + [P()] * 3 + [P(rows)]
    return jax.shard_map(
        local,
        mesh=mesh,
        in_specs=tuple(split),
        out_specs=(P(rows), P(rows), P(rows), P(), P(), P()),
        check_vma=False,
    )
```

```python
import math

import jax
import jax.numpy as jnp
from jax import lax
from jax.experimental import pallas as pl
from jax.experimental.pallas import tpu as pltpu
from jax.sharding import Mesh, PartitionSpec as P

BF = jnp.bfloat16
F32 = jnp.float32
TN = (((0,), (0,)), ((), ()))
NT = (((1,), (1,)), ((), ()))
NX, NZ, NY, NC = 4, 8, 8, 2
NG = NY * NC
BANDS = NX * NZ
SPARE_ROWS = 16
STORE = 8
FIRST = NZ * (2 * NX - 1)
VMEM = pl.BlockSpec(memory_space=pltpu.VMEM)
SMEM = pl.BlockSpec(memory_space=pltpu.SMEM)
HBM = pl.BlockSpec(memory_space=pltpu.HBM)


def sds(shape, dtype):
    return jax.ShapeDtypeStruct(shape, dtype)


def call(
    body, scalars, arrays, outs, out_specs=None, scratch=(), direct=(), extra=(), flops=0, vmem=63
):
    count, first = len(arrays), len(scalars)

    def kernel(*refs):
        sources = refs[first : first + count]
        rest = refs[first + count :]
        given, rest = rest[: len(direct)], rest[len(direct) + len(extra) :]
        outputs, rest = rest[: len(outs)], rest[len(outs) :]
        buffers, sems, rest = rest[:count], rest[count], rest[count + 1 :]
        copies = [
            pltpu.make_async_copy(source, buffer, sems.at[i])
            for i, (source, buffer) in enumerate(zip(sources, buffers, strict=True))
        ]
        for copy in copies:
            copy.start()
        body(refs[:first], buffers, copies, outputs, *([given] if direct else []), *rest)

    nbytes = sum(a.size * a.dtype.itemsize for a in (*arrays, *outs, *direct))
    return pl.pallas_call(
        kernel,
        out_shape=tuple(outs),
        in_specs=[SMEM] * first + [HBM] * (count + len(direct) + len(extra)),
        out_specs=tuple(out_specs or [VMEM] * len(outs)),
        scratch_shapes=[
            *(pltpu.VMEM(a.shape, a.dtype) for a in arrays),
            pltpu.SemaphoreType.DMA((max(count, 1),)),
            *scratch,
        ],
        compiler_params=pltpu.CompilerParams(vmem_limit_bytes=vmem << 20),
        cost_estimate=pl.CostEstimate(flops=flops, bytes_accessed=nbytes, transcendentals=0),
    )(*scalars, *arrays, *direct, *extra)


def wait(copies):
    for copy in copies:
        copy.wait()


def hot_columns(rows_ref, count_ref, g, nodes):
    rows = rows_ref[g : g + 1, :]
    lane = lax.broadcasted_iota(jnp.int32, rows.shape, 1)
    rows = jnp.where(lane < count_ref[0, g], rows, -1)
    node = lax.broadcasted_iota(jnp.int32, (nodes, rows.shape[1]), 0)
    return jnp.where(node == rows, 1.0, 0.0).astype(BF)


def pick_body(scalars, arrays, copies, outs):
    (count_ref,), (rows_ref, feat_ref), (out_ref,) = scalars, arrays, outs
    wait(copies)
    feat = feat_ref[...]
    for g in range(out_ref.shape[0]):
        hot = hot_columns(rows_ref, count_ref, g, feat.shape[0])
        out_ref[g] = lax.dot_general(hot, feat, TN, preferred_element_type=F32).astype(BF)


def spot_of(index_ref, t, k):
    index = index_ref[t, k]
    z, x = lax.shift_right_logical(index, 1) & (NZ - 1), lax.shift_right_logical(index, 4)
    return (z * NX + x) * 2 + (index & 1)


def tile_spot(index_ref, t, k):
    index = index_ref[t, k]
    z = lax.shift_right_logical(index, 1) & (NZ - 1)
    tile = lax.shift_right_logical(index, 4) * 2 + (index & 1)
    return jnp.where(tile == 2 * NX - 1, FIRST + z, z * (2 * NX - 1) + tile)


def main_body(
    scalars, arrays, copies, outs, gathered, tiles, acc, terms, tile_sem, term_sems
):
    index_ref, count_ref = scalars
    blocks_ref, outer_ref, pre_ref, w_ref, dout_ref, feat_ref, wself_ref, cut_ref = arrays
    out_ref, dagg_ref, back_ref, self_ref, term_ref = outs
    tile_copies = [
        pltpu.make_async_copy(gathered[0], tiles.at[pl.ds(0, FIRST)], tile_sem.at[0]),
        pltpu.make_async_copy(gathered[1], tiles.at[pl.ds(FIRST, NZ)], tile_sem.at[1]),
    ]
    for copy in tile_copies:
        copy.start()
    slots = blocks_ref.shape[1]
    spare = 2 * BANDS
    tiles[spare] = jnp.zeros(tiles.shape[1:], BF)

    def clear(i, carry):
        acc[i] = jnp.zeros(acc.shape[1:], F32)
        return carry

    lax.fori_loop(0, spare, clear, 0)
    wait(copies)
    wait(tile_copies)
    aggs, d_pres, d_aggs = [], [], []
    for t in range(2):
        rows = pl.ds(t * 128, 128)
        spots, term_spots = [
            [jnp.where(k < count_ref[t], spot(index_ref, t, k), spare) for k in range(slots)]
            for spot in (tile_spot, spot_of)
        ]
        total = outer_ref[rows, :]
        for k in range(0, slots, 2):
            left = jnp.concatenate([blocks_ref[t, k], blocks_ref[t, k + 1]], axis=1)
            right = jnp.concatenate([tiles[spots[k]], tiles[spots[k + 1]]], axis=0)
            total = total + jnp.dot(left, right, preferred_element_type=F32)
        agg = total.astype(BF)
        pre = pre_ref[rows, :] + jnp.dot(agg, w_ref[...], preferred_element_type=F32)
        sig = jax.nn.sigmoid(pre)
        out_ref[rows, :] = (pre * sig).astype(BF)
        d_pre = (dout_ref[rows, :].astype(F32) * sig * (1.0 + pre * (1.0 - sig))).astype(BF)
        d_agg = lax.dot_general(d_pre, w_ref[...], NT, preferred_element_type=F32).astype(BF)
        dagg_ref[rows, :] = d_agg
        for k in range(slots):
            term = lax.dot_general(blocks_ref[t, k], d_agg, TN, preferred_element_type=F32)
            acc[term_spots[k]] = acc[term_spots[k]] + term
        d_aggs.append(d_agg)
        aggs.append(agg)
        d_pres.append(d_pre)
    stores = []
    for c in range(STORE):
        part = pl.ds(c * (spare // STORE), spare // STORE)

        def convert(i, carry):
            terms[i] = acc[i].astype(BF)
            return carry

        lax.fori_loop(part.start, part.start + part.size, convert, 0)
        store = pltpu.make_async_copy(terms.at[part], term_ref.at[part], term_sems.at[c])
        store.start()
        stores.append(store)
    agg, d_pre = jnp.concatenate(aggs, axis=0), jnp.concatenate(d_pres, axis=0)
    width = d_pre.shape[1]
    groups = back_ref.shape[0]
    cut = cut_ref.shape[1] // groups
    share = 2 * width // groups
    for i, left in enumerate((feat_ref[...], agg)):
        grad = lax.dot_general(left, d_pre, TN, preferred_element_type=F32).astype(BF)
        for g in range(groups // 2):
            spot = i * groups // 2 + g
            back_ref[spot, pl.ds(cut, share), :] = grad[g * share : (g + 1) * share]
    bias = jnp.sum(d_pre.astype(F32), axis=0, keepdims=True)
    row = lax.broadcasted_iota(jnp.int32, (SPARE_ROWS, width), 0)
    bias = jnp.where(row == 0, bias, 0.0).astype(BF)
    for g in range(groups):
        back_ref[g, pl.ds(cut + share, SPARE_ROWS), :] = bias
    d_agg = jnp.concatenate(d_aggs, axis=0)
    for g in range(0, groups, 2):
        rows = lax.dot_general(
            cut_ref[:, pl.ds(g * cut, 2 * cut)], d_agg, TN, preferred_element_type=F32
        ).astype(BF)
        back_ref[g, pl.ds(0, cut), :] = rows[:cut]
        back_ref[g + 1, pl.ds(0, cut), :] = rows[cut:]
    self_ref[...] = lax.dot_general(d_pre, wself_ref[...], NT, preferred_element_type=F32)
    wait(stores)


def blocks_body(scalars, arrays, copies, outs):
    (index_ref, count_ref), (dagg_ref, first, last), (out_ref,) = scalars, arrays, outs
    wait(copies)
    for t in range(2):
        d_agg = dagg_ref[pl.ds(t * 128, 128), :]
        for k in range(out_ref.shape[1]):
            live = jnp.where(k < count_ref[t], 1.0, 0.0)
            spot = tile_spot(index_ref, t, k)
            tile = jnp.where(
                spot < FIRST, first[jnp.minimum(spot, FIRST - 1)], last[jnp.maximum(spot - FIRST, 0)]
            )
            grad = lax.dot_general(d_agg, tile, NT, preferred_element_type=F32)
            out_ref[t, k] = (grad * live).astype(BF)


def base_body(scalars, arrays, copies, outs):
    (count_ref,), (rows_ref, back_ref, self_ref), (out_ref,) = scalars, arrays, outs
    cut = rows_ref.shape[1]
    wait(copies)
    total = self_ref[...]
    for g in range(0, back_ref.shape[0], 2):
        hot = jnp.concatenate(
            [hot_columns(rows_ref, count_ref, g + i, total.shape[0]) for i in range(2)], axis=1
        )
        rows = jnp.concatenate([back_ref[g + i, pl.ds(0, cut), :] for i in range(2)], axis=0)
        total = total + jnp.dot(hot, rows, preferred_element_type=F32)
    out_ref[...] = total


def behind_body(scalars, arrays, copies, outs, returned, parts_ref, sem):
    rows = parts_ref.shape[1]
    first = returned[0].shape[1] - rows
    copy = pltpu.make_async_copy(returned[0].at[:, pl.ds(first, rows)], parts_ref, sem)
    copy.start()
    sum_body(scalars, (parts_ref,), [copy], outs)


def sum_body(scalars, arrays, copies, outs):
    (parts_ref,), (out_ref,) = arrays, outs
    wait(copies)
    total = parts_ref[0].astype(F32)
    for i in range(1, parts_ref.shape[0]):
        total = total + parts_ref[i].astype(F32)
    for i in range(out_ref.shape[0]):
        out_ref[i] = total.astype(BF)


def a2a(x, axis):
    return lax.all_to_all(x, axis, 0, 0, tiled=True)


def shift(x, axis, n, by):
    return lax.ppermute(x, axis, [(i, (i + by) % n) for i in range(n)])


def local(
    features, block_index, block_count, block_values, cut_weight, send_rows, send_count,
    w_self, w_neigh, bias, d_out,
):
    nodes, width = features.shape
    tiles_here, slots = block_index.shape
    scale = 1.0 / math.sqrt(nodes * NG * BANDS)
    rows2 = send_rows.reshape(NG, -1)
    cut = rows2.shape[1]
    node_bf, node_f32 = sds((nodes, width), BF), sds((nodes, width), F32)
    cut_bf = sds((NG, cut, width), BF)

    along_x = lax.all_gather(features, "x", axis=0, tiled=True)
    gathered = [
        lax.all_gather(rows, "z", axis=0, tiled=True).reshape(-1, 128, width)
        for rows in (along_x[:-128], along_x[-128:])
    ]

    (outgoing,) = call(
        pick_body, [send_count], [rows2, features], [cut_bf], flops=2 * NG * cut * width * nodes,
    )
    arrived = a2a(outgoing, ("y", "c")).reshape(NG * cut, width)
    outer = jnp.dot(cut_weight, arrived, preferred_element_type=F32)
    own_pre = jnp.dot(features, w_self, preferred_element_type=F32) + bias

    share = 2 * width // NG
    outs = [
        node_bf, node_bf, sds((NG, cut + share + SPARE_ROWS, width), BF), node_f32,
        sds((2 * BANDS, 128, width), BF),
    ]
    spared = (2 * BANDS + 1, 128, width)
    output, d_agg, back, self_back, terms = call(
        main_body,
        [block_index, block_count],
        [block_values, outer, own_pre, w_neigh, d_out, features, w_self, cut_weight],
        outs,
        out_specs=[VMEM] * (len(outs) - 1) + [HBM],
        scratch=[
            pltpu.VMEM(spared, BF),
            pltpu.VMEM(spared, F32),
            pltpu.VMEM((2 * BANDS, 128, width), BF),
            pltpu.SemaphoreType.DMA((2,)),
            pltpu.SemaphoreType.DMA((STORE,)),
        ],
        direct=gathered,
        flops=1 << 30,
    )

    terms = lax.psum_scatter(terms.reshape(NZ, NX * nodes, width), "z", scatter_dimension=0)
    terms = terms.reshape(NX, nodes, width)
    me = lax.axis_index("x")

    returned = a2a(back, ("y", "c"))
    (grad_blocks,) = call(
        blocks_body, [block_index, block_count], [d_agg, *gathered], [sds(block_values.shape, BF)],
        flops=2 * tiles_here * slots * 128 * 128 * width,
    )
    (part,) = call(
        behind_body, [], [], [sds((NX, share + SPARE_ROWS, width), BF)],
        scratch=[pltpu.VMEM((NG, share + SPARE_ROWS, width), BF), pltpu.SemaphoreType.DMA],
        direct=[returned], extra=[grad_blocks],
    )
    part = a2a(part, "x")
    part = jnp.sum(part.astype(F32), axis=0).astype(BF)
    part = a2a(jnp.broadcast_to(part[None], (NZ, *part.shape)), "z")
    moved = []
    for by in range(NX):
        rows = lax.dynamic_index_in_dim(terms, (me + by) & (NX - 1), 0, keepdims=False)
        moved.append(shift(rows, "x", NX, by) if by else rows)
    (base,) = call(
        base_body, [send_count], [rows2, returned, self_back], [node_f32],
        flops=2 * NG * cut * width * nodes,
    )
    (part,) = call(
        sum_body, [], [part], [sds((NY, share + SPARE_ROWS, width), BF)], extra=[terms]
    )
    part = a2a(part, "y")
    grads = lax.all_gather(part, "c", axis=1).reshape(NG, share + SPARE_ROWS, width)
    grads = grads.astype(F32) * scale
    weight_grads = grads[:, :share].reshape(2, width, width)

    d_features = (base + sum(rows.astype(F32) for rows in moved)).astype(BF)

    return (
        output,
        d_features,
        grad_blocks,
        weight_grads[0],
        weight_grads[1],
        grads[0, share],
    )


def solution(mesh):
    mesh = Mesh(mesh.devices.reshape(NY, NC, NX, NZ), ("y", "c", "x", "z"))
    rows = ("y", "c", "x", "z")
    split = [P(rows)] * 7 + [P()] * 3 + [P(rows)]
    return jax.shard_map(
        local,
        mesh=mesh,
        in_specs=tuple(split),
        out_specs=(P(rows), P(rows), P(rows), P(), P(), P()),
        check_vma=False,
    )
```
